32 devices in a mesh: lead: 4 (over y, x), lat: 8 (over z, core).
Axes of the slice: x: 2, y: 2, z: 4, core: 2. Of those that a mesh axis runs over, the one named last changes fastest.
Arguments:
- state: float32 [4, 2, 144, 192, 256], P('lead', None, 'lat'), may hold values from -6 to 6
- earlier: float32 [4, 2, 144, 192, 256], P('lead', None, 'lat'), may hold values from -6 to 6
- cotangent: float32 [4, 2, 144, 192, 256], P('lead', None, 'lat'), may hold values from -6 to 6
- level_mask: int32 [4, 2, 144, 192], P('lead', None, 'lat'), may hold values from 0 to 1, as said below
- window_offsets: int32 [4, 2], P('lead'), may hold values from 1 to 11, as said below
- lead_index: int32 [4], P('lead'), may hold values from 0 to 15
- embeddings: float32 [16, 256], replicated, may hold values from -6 to 6
- w_mod: float32 [256, 512], replicated, may hold values from -0.1875 to 0.1875
- b_mod: float32 [512], replicated, may hold values from -4 to 4
- w_qkv: bfloat16 [256, 768], replicated, may hold values from -0.375 to 0.375
- bias_table: float32 [8, 759], replicated, may hold values from -6 to 6
- w_out: bfloat16 [256, 256], replicated, may hold values from -1 to 1
- b_out: float32 [256], replicated, may hold values from -4 to 4
- norm_gain: float32 [256], replicated, may hold values from 0.25 to 1.75
- norm_bias: float32 [256], replicated, may hold values from -4 to 4
- w_up: bfloat16 [256, 1024], replicated, may hold values from -0.375 to 0.375
- b_up: float32 [1024], replicated, may hold values from -6 to 6
- w_down: bfloat16 [1024, 256], replicated, may hold values from -0.375 to 0.375
- b_down: float32 [256], replicated, may hold values from -4 to 4
Outputs:
- block_out: float32 [4, 2, 144, 192, 256], P('lead', None, 'lat')
- state_grad: float32 [4, 2, 144, 192, 256], P('lead', None, 'lat')
- grad_w_mod: float32 [256, 512], replicated
- grad_b_mod: float32 [512], replicated
- grad_w_qkv: float32 [256, 768], replicated
- grad_bias_table: float32 [8, 759], replicated
- grad_w_out: float32 [256, 256], replicated
- grad_b_out: float32 [256], replicated
- grad_norm_gain: float32 [256], replicated
- grad_norm_bias: float32 [256], replicated
- grad_w_up: float32 [256, 1024], replicated
- grad_b_up: float32 [1024], replicated
- grad_w_down: float32 [1024, 256], replicated
- grad_b_down: float32 [256], replicated
The draws below stay inside these ranges and needn't reach their ends.
Inputs may be any that keep to these rules, and one draw needn't show every extreme that they name: `level_mask`: level 0 tokens are always present; a token of another level is present with probability 0.7. `window_offsets`: column 0 holds latitude offsets of 1 to 5, column 1 longitude offsets of 1 to 11; the top end is taken by some lead time.
All inputs are finite; a program needn't handle non-finite values.
Results may differ from the reference program's by a relative error of at most 0.012.
The reference program's roundings to bfloat16 on the way count: a program that leaves them out, or rounds other values in their place, can miss the bound.
Values sent between devices are 32-bit elements; how exact they have to be, the bound alone decides.
A program may use at most 384 MiB of HBM per device.

```python
import jax
import jax.numpy as jnp
import numpy as np
from jax import lax

D = 256
HEADS = 8
FF = 1024
LEVELS = 2
WLAT = 6
WLON = 12
NEMB = 16
LON = 192
LEADS = 4
LAT = 144
BIAS_ROWS = 759


def draw_level_mask(key, part):
    key = jax.random.fold_in(key, 1)
    upper = (jax.random.randint(key, (LEADS, LEVELS - 1, LAT, LON), 0, 10) < 7).astype(jnp.int32)
    ground = jnp.ones((LEADS, 1, LAT, LON), jnp.int32)
    return jnp.concatenate([ground, upper], axis=1)


def draw_window_offsets(key, part):
    key = jax.random.fold_in(key, 2)
    key_one, key_two, key_three, key_four = jax.random.split(key, 4)
    lat_off = jax.random.randint(key_one, (LEADS,), 1, WLAT)
    lon_off = jax.random.randint(key_two, (LEADS,), 1, WLON)
    pick_one = jax.random.randint(key_three, (), 0, LEADS)
    pick_two = jax.random.randint(key_four, (), 0, LEADS)
    positions = jnp.arange(LEADS)
    lat_off = jnp.where(positions == pick_one, WLAT - 1, lat_off)
    lon_off = jnp.where(positions == pick_two, WLON - 1, lon_off)
    return jnp.stack([lat_off, lon_off], axis=1).astype(jnp.int32)


def plant(drawn, stream_key, smallest, top_value):
    place = [jax.random.randint(jax.random.fold_in(stream_key, axis), (), 0, length) for axis, length in enumerate(drawn.shape)]
    main_axis = drawn.shape.index(max(drawn.shape))
    next_to = place[:main_axis] + [(place[main_axis] + 1) % drawn.shape[main_axis]] + place[main_axis + 1:]
    return drawn.at[tuple(place)].set(smallest).at[tuple(next_to)].set(top_value)


def steps_of(key, extent, pieces, low, largest):
    gain = 1.0
    for position, parts in pieces:
        steps = jax.random.uniform(jax.random.fold_in(jax.random.fold_in(key, 6), position), (parts,), jnp.float32, low / len(pieces), largest / len(pieces))
        gain = gain * jnp.repeat(jnp.exp(steps), extent[position] // parts).reshape((-1,) + (1,) * (len(extent) - 1 - position))
    return gain


def gaussian(key, extent, scale, limit, cuts=(), held_as=jnp.bfloat16):
    result = jax.random.normal(key, extent, jnp.float32) * scale
    if len(cuts) > 0:
        result = steps_of(key, extent, cuts, -0.22, 0.18) * result
    return jnp.clip(result, min=-limit, max=limit).astype(held_as)


def setup_inputs(seed: int = 0) -> dict:
    keys = jax.random.split(jax.random.key(seed), 20)
    state = gaussian(keys[0], (LEADS, LEVELS, LAT, LON, D), 1.0, 6.0, ((0, 4), (2, 8)), jnp.float32)
    earlier = gaussian(keys[1], (LEADS, LEVELS, LAT, LON, D), 1.0, 6.0, ((0, 4), (2, 8)), jnp.float32)
    cotangent = gaussian(keys[2], (LEADS, LEVELS, LAT, LON, D), 1.0, 6.0, ((0, 4), (2, 8)), jnp.float32)
    level_mask = draw_level_mask(jax.random.fold_in(keys[19], 71), 0)
    window_offsets = draw_window_offsets(jax.random.fold_in(keys[19], 71), 0)
    lead_index = plant(jax.random.randint(keys[5], (LEADS,), 0, NEMB), jax.random.fold_in(keys[5], 1), 0, NEMB - 1).astype(jnp.int32)
    embeddings = gaussian(keys[6], (NEMB, D), 1.0, 6.0, (), jnp.float32)
    w_mod = gaussian(keys[7], (D, 2 * D), (4 * D) ** -0.5, 0.1875, (), jnp.float32)
    b_mod = gaussian(keys[8], (2 * D,), 0.3, 4.0, (), jnp.float32)
    w_qkv = gaussian(keys[9], (D, 3 * D), D ** -0.5, 0.375)
    bias_table = gaussian(keys[10], (HEADS, BIAS_ROWS), 1.0, 6.0, (), jnp.float32)
    w_out = gaussian(keys[11], (D, D), (D // 8) ** -0.5, 1.0)
    b_out = gaussian(keys[12], (D,), 0.3, 4.0, (), jnp.float32)
    norm_gain = jnp.clip(1.0 + 0.15 * jax.random.normal(keys[13], (D,), jnp.float32), 0.25, 1.75)
    norm_bias = gaussian(keys[14], (D,), 0.3, 4.0, (), jnp.float32)
    w_up = gaussian(keys[15], (D, FF), D ** -0.5, 0.375)
    b_up = gaussian(keys[16], (FF,), 0.5, 6.0, (), jnp.float32)
    w_down = gaussian(keys[17], (FF, D), (FF // 4) ** -0.5, 0.375)
    b_down = gaussian(keys[18], (D,), 0.3, 4.0, (), jnp.float32)
    return dict(state=state, earlier=earlier, cotangent=cotangent, level_mask=level_mask, window_offsets=window_offsets, lead_index=lead_index, embeddings=embeddings, w_mod=w_mod, b_mod=b_mod, w_qkv=w_qkv, bias_table=bias_table, w_out=w_out, b_out=b_out, norm_gain=norm_gain, norm_bias=norm_bias, w_up=w_up, b_up=b_up, w_down=w_down, b_down=b_down)


EPS = 1e-06
NEG = -1000000000.0
HIGH = lax.Precision.HIGHEST

@jax.custom_vjp
def low(v):
    return lax.optimization_barrier(v.astype(jnp.bfloat16)).astype(jnp.float32)

@jax.custom_vjp
def low_back(v):
    return v

def low_keep(v):
    return (low(v), None)

def low_pass(kept, grad):
    return (grad,)

def back_keep(v):
    return (v, None)

def back_low(kept, grad):
    return (low(grad),)
low.defvjp(low_keep, low_pass)
low_back.defvjp(back_keep, back_low)

def relative_index():
    level_ids, row_ids, col_ids = np.meshgrid(np.arange(LEVELS), np.arange(WLAT), np.arange(WLON), indexing='ij')
    level_ids = level_ids.reshape(-1)
    row_ids = row_ids.reshape(-1)
    col_ids = col_ids.reshape(-1)
    span_row = 2 * WLAT - 1
    span_col = 2 * WLON - 1
    level_part = (level_ids[:, None] - level_ids[None, :] + LEVELS - 1) * span_row * span_col
    row_part = (row_ids[:, None] - row_ids[None, :] + WLAT - 1) * span_col
    col_part = col_ids[:, None] - col_ids[None, :] + WLON - 1
    return (level_part + row_part + col_part).astype(np.int32)

def window_tokens(grid):
    shape = grid.shape
    rest = shape[3:]
    blocks = grid.reshape((shape[0], shape[1] // WLAT, WLAT, shape[2] // WLON, WLON) + rest)
    order = (1, 3, 0, 2, 4) + tuple(range(5, 5 + len(rest)))
    return blocks.transpose(order).reshape((-1, LEVELS * WLAT * WLON) + rest)

def grid_tokens(windows, lat_rows, lon_cols):
    rest = windows.shape[2:]
    blocks = windows.reshape((lat_rows // WLAT, lon_cols // WLON, LEVELS, WLAT, WLON) + rest)
    order = (2, 0, 3, 1, 4) + tuple(range(5, 5 + len(rest)))
    return blocks.transpose(order).reshape((LEVELS, lat_rows, lon_cols) + rest)

def normalize(tokens):
    mean_val = lax.optimization_barrier(jnp.mean(tokens, axis=-1, keepdims=True))
    centered = tokens - mean_val
    return centered * lax.rsqrt(lax.optimization_barrier(jnp.mean(centered * centered, axis=-1, keepdims=True)) + EPS)

def lead_block(params, pack):
    w_mod, b_mod, w_qkv, bias_table, w_out, b_out, norm_gain, norm_bias, w_up, b_up, w_down, b_down = params
    grid_in, grid_mask, offsets, emb_row = pack
    lat_total = grid_in.shape[1]
    lon_total = grid_in.shape[2]
    width = grid_in.shape[3]
    head_size = width // HEADS
    row_index = (jnp.arange(lat_total, dtype=jnp.int32) + offsets[0]) % lat_total
    col_index = (jnp.arange(lon_total, dtype=jnp.int32) + offsets[1]) % lon_total
    rolled = grid_in[:, row_index][:, :, col_index]
    live_grid = grid_mask[:, row_index][:, :, col_index]
    tokens = window_tokens(rolled)
    live = window_tokens(live_grid) == 1
    windows, span = (tokens.shape[0], tokens.shape[1])
    modulation = jnp.dot(emb_row, w_mod, precision=HIGH) + b_mod
    ln_in = low(normalize(tokens) * (1.0 + modulation[width:]) + modulation[:width])
    projected = low_back(low(jnp.einsum('wtd,de->wte', ln_in, w_qkv, precision=HIGH)))
    split = projected.reshape(windows, span, 3, HEADS, head_size)
    queries = split[:, :, 0]
    key_vals = split[:, :, 1]
    value_vals = split[:, :, 2]
    raw = low_back(jnp.einsum('wqhd,wkhd->whqk', queries, key_vals, precision=HIGH))
    bias_full = bias_table[:, relative_index()]
    scores = raw * head_size ** (-0.5) + bias_full[None]
    scores = jnp.where(live[:, None, None, :], scores, NEG)
    peak = lax.optimization_barrier(jnp.max(scores, axis=-1, keepdims=True))
    expo = jnp.exp(scores - peak)
    weights = low(expo / lax.optimization_barrier(jnp.sum(expo, axis=-1, keepdims=True)))
    attended = jnp.einsum('whqk,wkhd->wqhd', weights, value_vals, precision=HIGH).reshape(windows, span, width)
    attended = low_back(low(attended))
    branch = low_back(jnp.einsum('wtd,de->wte', attended, w_out, precision=HIGH) + b_out)
    mid = tokens + branch
    ln_two = low(normalize(mid) * norm_gain + norm_bias)
    hidden = low_back(jnp.einsum('wtd,df->wtf', ln_two, w_up, precision=HIGH) + b_up)
    activ = low(jax.nn.gelu(hidden))
    out_tokens = mid + low_back(jnp.einsum('wtf,fd->wtd', activ, w_down, precision=HIGH) + b_down)
    out_grid = grid_tokens(out_tokens, lat_total, lon_total)
    back_rows = (jnp.arange(lat_total, dtype=jnp.int32) - offsets[0]) % lat_total
    back_cols = (jnp.arange(lon_total, dtype=jnp.int32) - offsets[1]) % lon_total
    return out_grid[:, back_rows][:, :, back_cols]

def reference(state, earlier, cotangent, level_mask, window_offsets, lead_index, embeddings, w_mod, b_mod, w_qkv, bias_table, w_out, b_out, norm_gain, norm_bias, w_up, b_up, w_down, b_down):
    emb_rows = embeddings[lead_index.astype(jnp.int32)]
    params = (w_mod, b_mod, w_qkv.astype(jnp.float32), bias_table, w_out.astype(jnp.float32), b_out, norm_gain, norm_bias, w_up.astype(jnp.float32), b_up, w_down.astype(jnp.float32), b_down)

    def forward(state_in, params_in):
        inputs = jnp.roll(state_in, 1, axis=0) + earlier
        checked = jax.checkpoint(lead_block)
        return lax.map(lambda pack: checked(params_in, pack), (inputs, level_mask, window_offsets, emb_rows))
    block_out, pullback = jax.vjp(forward, state, params)
    state_grad, grads = pullback(cotangent)
    return (block_out, state_grad) + tuple(grads)
```

```python
import functools

import jax
import jax.numpy as jnp
import numpy as np
from jax import lax
from jax.experimental import pallas as pl
from jax.experimental.pallas import tpu as pltpu
from jax.sharding import PartitionSpec as P

HEADS = 8
LEVELS = 2
WLAT = 6
WLON = 12
SPAN = LEVELS * WLAT * WLON
MARGIN = WLAT - 1
SPAN_ROW = 2 * WLAT - 1
SPAN_COL = 2 * WLON - 1
TABLE_ROWS = (2 * LEVELS - 1) * SPAN_ROW * SPAN_COL
TABLE_PAD = 768
TILE = 128
REST = SPAN - TILE
LOG2E = 1.4426950408889634
GELU_ONE = 0.7978845608028654
GELU_TWO = GELU_ONE * 0.044715
REACH = 24
BLOCK = 48
WIDE = 512

EPS = 1e-06
NEG = -1000000000.0
HIGH = lax.Precision.HIGHEST
F32 = jnp.float32
BF16 = jnp.bfloat16
VMEM = pltpu.VMEM
WHOLE = pl.BlockSpec(memory_space=pltpu.VMEM)
SMEM = pl.BlockSpec(memory_space=pltpu.SMEM)
ANYWHERE = pl.BlockSpec(memory_space=pl.ANY)
SMALL = pl.CostEstimate(flops=1, bytes_accessed=1, transcendentals=0)
LIMIT = 30 * 1024 * 1024
BLOCK_LIMIT = 48 * 1024 * 1024


def passed_along(value, axis, steps):
    count = lax.axis_size(axis)
    pairs = [(source, (source + steps) % count) for source in range(count)]
    return lax.ppermute(value, axis, pairs)


def in_hbm(array):
    return pltpu.with_memory_space_constraint(array, pltpu.HBM)


def dot_nn(a, b):
    return lax.dot_general(a, b, (((1,), (0,)), ((), ())), preferred_element_type=F32)


def prepare_kernel(count, table_ref, *refs):
    out_ref, scratch = refs[-count - 2], refs[-1]
    for source, target in zip(refs[:count], refs[-count - 1 : -1]):
        target[...] = source[...].T
    table = table_ref[...]
    lanes = lax.broadcasted_iota(jnp.int32, (384, SPAN), 0)
    cell = lax.broadcasted_iota(jnp.int32, (384, SPAN), 1)
    place = (
        (cell // (WLAT * WLON)) * (SPAN_ROW * SPAN_COL)
        + ((cell // WLON) % WLAT) * SPAN_COL
        + cell % WLON
    )
    pick = (lanes == place).astype(F32)
    base = (SPAN_ROW * SPAN_COL) * (LEVELS - 1) + SPAN_COL * (WLAT - 1) + WLON - 1
    for group in range(LEVELS * WLAT):
        level, row = divmod(group, WLAT)
        start = level * SPAN_ROW * SPAN_COL + row * SPAN_COL - group * WLON - base
        moved = pltpu.roll(table, start % TABLE_PAD, 1)
        for head in range(HEADS):
            scratch[head, pl.ds(group * WLON, WLON), :] = jnp.broadcast_to(
                moved[head : head + 1], (WLON, TABLE_PAD)
            )
    for head in range(HEADS):
        rows = pltpu.roll(scratch[head], 0, 1, stride=1, stride_axis=0)
        values = jnp.dot(rows[:, :384], pick, precision=HIGH, preferred_element_type=F32) * LOG2E
        out_ref[:, pl.ds(head * TILE, TILE)] = values[:, :TILE]
        out_ref[:, pl.ds(HEADS * TILE + head * REST, REST)] = values[:, TILE:]


def prepare(bias_table, weights, after):
    padded = jnp.pad(bias_table, ((0, 0), (0, TABLE_PAD - TABLE_ROWS)))
    return pl.pallas_call(
        functools.partial(prepare_kernel, len(weights)),
        out_shape=[jax.ShapeDtypeStruct((SPAN, HEADS * SPAN), F32)]
        + [jax.ShapeDtypeStruct(array.shape[::-1], array.dtype) for array in weights],
        in_specs=[WHOLE] * (1 + len(weights)) + [ANYWHERE] * len(after),
        out_specs=[WHOLE] * (1 + len(weights)),
        scratch_shapes=[VMEM((HEADS, SPAN, TABLE_PAD), F32)],
        compiler_params=pltpu.CompilerParams(vmem_limit_bytes=LIMIT),
        cost_estimate=SMALL,
        name="prepare",
    )(padded, *weights, *after)


def collect_kernel(first, width, leads, lead_ref, grad_ref, small_ref, *refs):
    out_ref, extra, sem = refs[-3:]
    cell = lax.broadcasted_iota(jnp.int32, (SPAN, TABLE_PAD), 0)
    lanes = lax.broadcasted_iota(jnp.int32, (SPAN, TABLE_PAD), 1)
    place = (
        (cell // (WLAT * WLON)) * (SPAN_ROW * SPAN_COL)
        + ((cell // WLON) % WLAT) * SPAN_COL
        + cell % WLON
    )
    base = (SPAN_ROW * SPAN_COL) * (LEVELS - 1) + SPAN_COL * (WLAT - 1) + WLON - 1
    spread = (lanes == base - place).astype(F32)
    extra[...] = jnp.zeros_like(extra)
    count = small_ref.shape[1] // width
    sums = jnp.sum(small_ref[...], axis=0, keepdims=True)
    for index in range(count):
        extra[pl.ds(index, 1), :] = sums[:, index * width : (index + 1) * width]
    at = count
    for head in range(HEADS):
        parts = [
            grad_ref[:, pl.ds(head * TILE, TILE)],
            grad_ref[:, pl.ds(HEADS * TILE + head * REST, REST)],
        ]
        wide = jnp.dot(
            jnp.concatenate(parts, axis=1), spread, precision=HIGH, preferred_element_type=F32
        )
        wide = pltpu.roll(wide, 0, 1, stride=1, stride_axis=0)
        total = None
        for group in range(LEVELS * WLAT):
            level, row = divmod(group, WLAT)
            start = level * SPAN_ROW * SPAN_COL + row * SPAN_COL - group * WLON
            part = jnp.sum(wide[group * WLON : (group + 1) * WLON], axis=0, keepdims=True)
            part = pltpu.roll(jnp.broadcast_to(part, (8, TABLE_PAD)), start % TABLE_PAD, 1)
            total = part if total is None else total + part
        for index in range(TABLE_PAD // width):
            extra[pl.ds(at, 1), :] = total[0:1, index * width : (index + 1) * width]
            at += 1
    for index in range(2):
        value = sums[:, (4 + index) * width : (5 + index) * width]
        extra[pl.ds(at + leads * index + lead_ref[0], 1), :] = value
    copy = pltpu.make_async_copy(extra, out_ref.at[pl.ds(first, extra.shape[0]), :], sem)
    copy.start()
    copy.wait()


def collect(lead_index, leads, bias, small, buffer, first, after):
    rows, width = buffer.shape
    return pl.pallas_call(
        functools.partial(collect_kernel, first, width, leads),
        out_shape=jax.ShapeDtypeStruct(buffer.shape, F32),
        in_specs=[SMEM, WHOLE, WHOLE, ANYWHERE] + [ANYWHERE] * len(after),
        out_specs=ANYWHERE,
        scratch_shapes=[VMEM((rows - first, width), F32), pltpu.SemaphoreType.DMA],
        input_output_aliases={3: 0},
        compiler_params=pltpu.CompilerParams(vmem_limit_bytes=LIMIT),
        cost_estimate=SMALL,
        name="collect",
    )(lead_index, bias, small, buffer, *after)


class Peers:
    def __init__(self, lats, leads, rows, send_sems, got_sems):
        self.lead = lax.axis_index("lead")
        lat = lax.axis_index("lat")
        self.core = lax.rem(lat, 2)
        self.chip = lax.div(lat, 2)
        self.chips, self.leads = lats // 2, leads
        self.half = rows // 2
        self.part = self.half // self.chips
        self.piece = self.part // leads
        self.pair = (self.lead, lat + 1 - 2 * self.core)
        self.along_lat = [
            (self.lead, 2 * lax.rem(self.chip + d, self.chips) + self.core)
            for d in range(1, self.chips)
        ]
        self.along_lead = [(lax.rem(self.lead + d, leads), lat) for d in range(1, leads)]
        self.sems = (send_sems, got_sems)
        self.count = 0

    def meet(self, peers):
        barrier = pltpu.get_barrier_semaphore()
        for peer in peers:
            pl.semaphore_signal(
                barrier, inc=1, device_id=peer, device_id_type=pl.DeviceIdType.MESH
            )
        pl.semaphore_wait(barrier, len(peers))

    def send(self, source, target, peer):
        copy = pltpu.make_async_remote_copy(
            src_ref=source,
            dst_ref=target,
            send_sem=self.sems[0].at[self.count],
            recv_sem=self.sems[1].at[self.count],
            device_id=peer,
            device_id_type=pl.DeviceIdType.MESH,
        )
        self.count += 1
        copy.start()
        return copy


def some_rows(start, size):
    return pl.ds(pl.multiple_of(start, 8), size)


def scatter_kernel(lats, leads, in_ref, *refs):
    out_ref, got_pair, sum_pair, got_lat, sum_lat, got_lead, send_sems, got_sems = refs[-8:]
    at = Peers(lats, leads, in_ref.shape[0], send_sems, got_sems)
    at.meet([at.pair] + at.along_lat + at.along_lead)
    at.send(in_ref.at[some_rows((1 - at.core) * at.half, at.half), :], got_pair, at.pair).wait()
    sum_pair[...] = in_ref[some_rows(at.core * at.half, at.half), :] + got_pair[...]
    copies = [
        at.send(
            sum_pair.at[some_rows(lax.rem(at.chip + d, at.chips) * at.part, at.part), :],
            got_lat.at[d - 1],
            at.along_lat[d - 1],
        )
        for d in range(1, at.chips)
    ]
    for copy in copies:
        copy.wait()
    total = sum_pair[some_rows(at.chip * at.part, at.part), :]
    for d in range(1, at.chips):
        total = total + got_lat[d - 1]
    sum_lat[...] = total
    copies = [
        at.send(
            sum_lat.at[some_rows(lax.rem(at.lead + d, leads) * at.piece, at.piece), :],
            got_lead.at[d - 1],
            at.along_lead[d - 1],
        )
        for d in range(1, leads)
    ]
    for copy in copies:
        copy.wait()
    mine = some_rows(at.lead * at.piece, at.piece)
    total = sum_lat[mine, :]
    for d in range(1, leads):
        total = total + got_lead[d - 1]
    out_ref[mine, :] = total
    copies = [at.send(out_ref.at[mine, :], out_ref.at[mine, :], peer) for peer in at.along_lead]
    for copy in copies:
        copy.wait()


def scattered_sum(buffer, after):
    rows, width = buffer.shape
    lats = lax.axis_size("lat")
    leads = lax.axis_size("lead")
    chips = lats // 2
    half = rows // 2
    part = half // chips
    piece = part // leads
    copies = chips + 2 * leads - 2
    return pl.pallas_call(
        functools.partial(scatter_kernel, lats, leads),
        out_shape=jax.ShapeDtypeStruct((part, width), F32),
        in_specs=[WHOLE] + [ANYWHERE] * len(after),
        out_specs=WHOLE,
        scratch_shapes=[
            VMEM((half, width), F32),
            VMEM((half, width), F32),
            VMEM((chips - 1, part, width), F32),
            VMEM((part, width), F32),
            VMEM((leads - 1, piece, width), F32),
            pltpu.SemaphoreType.DMA((copies,)),
            pltpu.SemaphoreType.DMA((copies,)),
        ],
        compiler_params=pltpu.CompilerParams(
            vmem_limit_bytes=LIMIT, collective_id=0, has_side_effects=True
        ),
        cost_estimate=SMALL,
        name="scattered_sum",
    )(buffer, *after)


def hold_kernel(count, *refs):
    for source, target in zip(refs[:count], refs[-count:]):
        target[...] = source[...]


def held_until(arrays, after):
    return pl.pallas_call(
        functools.partial(hold_kernel, len(arrays)),
        out_shape=[jax.ShapeDtypeStruct(array.shape, F32) for array in arrays],
        in_specs=[WHOLE] * len(arrays) + [ANYWHERE] * len(after),
        out_specs=[WHOLE] * len(arrays),
        compiler_params=pltpu.CompilerParams(vmem_limit_bytes=LIMIT),
        cost_estimate=SMALL,
        name="hold",
    )(*arrays, *after)


def gathered(part, after):
    lats = lax.axis_size("lat")
    far = [passed_along(part, "lat", 2 * d) for d in range(1, lats // 2)]
    own = [part] + list(held_until(far, after))
    pairs = [(source, source ^ 1) for source in range(lats)]
    return own, [lax.ppermute(array, "lat", pairs) for array in own]


def finish_kernel(chips, hidden, embed_rows, place_ref, embed_ref, *refs):
    parts, others = refs[:chips], refs[chips : 2 * chips]
    outs, buffer = refs[2 * chips : -1], refs[-1]
    part, width = parts[0].shape
    core, chip = place_ref[0], place_ref[1]
    for index in range(chips):
        at = lax.rem(chip + chips - index, chips) * part
        buffer[some_rows(core * (chips * part) + at, part), :] = parts[index][...]
        buffer[some_rows((1 - core) * (chips * part) + at, part), :] = others[index][...]
    g_mod, g_b_mod, g_qkv, g_table, g_out, g_b_out, g_gain, g_bias, g_up, g_b_up, g_down, g_b_down = outs
    for index in range(3):
        lanes = slice(index * width, (index + 1) * width)
        g_qkv[:, lanes] = buffer[index * width : (index + 1) * width, :]
    g_out[...] = buffer[3 * width : 4 * width, :]
    for index in range(hidden // width):
        lanes = slice(index * width, (index + 1) * width)
        at = 4 * width + index * width
        g_up[:, lanes] = buffer[at : at + width, :]
        at += hidden
        g_down[lanes, :] = buffer[at : at + width, :].T
    at = 4 * width + 2 * hidden
    for place, (target, index) in enumerate(
        [(g_b_down, 0), (g_gain, 0), (g_bias, 0), (g_b_out, 0), (g_b_mod, 0), (g_b_mod, 1)]
        + [(g_b_up, index) for index in range(hidden // width)]
    ):
        target[:, index * width : (index + 1) * width] = buffer[at + place : at + place + 1, :]
    at += 6 + hidden // width
    each = TABLE_PAD // width
    heads = []
    for head in range(HEADS):
        first = at + head * each
        heads.append(
            jnp.concatenate([buffer[first + i : first + i + 1, :] for i in range(each)], axis=1)
        )
    before = lax.broadcasted_iota(jnp.int32, (TABLE_PAD, TABLE_PAD), 0)
    behind = lax.broadcasted_iota(jnp.int32, (TABLE_PAD, TABLE_PAD), 1)
    turn = (before + behind == TABLE_ROWS - 1).astype(F32)
    turned = jnp.dot(
        jnp.concatenate(heads, axis=0), turn, precision=HIGH, preferred_element_type=F32
    )
    g_table[...] = turned[:, :TABLE_ROWS]
    at += HEADS * each
    for index in range(2):
        lanes = slice(index * width, (index + 1) * width)
        rows = buffer[at + index * embed_rows : at + (index + 1) * embed_rows, :]
        g_mod[:, lanes] = jnp.dot(
            embed_ref[...], rows, precision=HIGH, preferred_element_type=F32
        )


def finished(own, others, embeddings, width, hidden):
    chips = len(own)
    lat = lax.axis_index("lat")
    place = jnp.stack([lat % 2, lat // 2]).astype(jnp.int32)
    shapes = [(width, 2 * width), (1, 2 * width), (width, 3 * width), (HEADS, TABLE_ROWS)]
    shapes += [(width, width), (1, width), (1, width), (1, width), (width, hidden), (1, hidden)]
    shapes += [(hidden, width), (1, width)]
    outs = pl.pallas_call(
        functools.partial(finish_kernel, chips, hidden, embeddings.shape[0]),
        out_shape=[jax.ShapeDtypeStruct(shape, F32) for shape in shapes],
        in_specs=[SMEM] + [WHOLE] * (1 + 2 * chips),
        out_specs=[WHOLE] * len(shapes),
        scratch_shapes=[VMEM((2 * chips * own[0].shape[0], width), F32)],
        compiler_params=pltpu.CompilerParams(vmem_limit_bytes=LIMIT),
        cost_estimate=SMALL,
        name="finish",
    )(place, embeddings.T, *own, *others)
    return tuple(out.reshape(-1) if out.shape[0] == 1 else out for out in outs)


def roll_kernel(specs, rows, *refs):
    offsets, own = refs[0], refs[1]
    sems = refs[-1]
    grids = refs[-1 - len(specs) : -1]
    outs = refs[-1 - 2 * len(specs) : -1 - len(specs)]
    copies = []
    for spec, grid in zip(specs, grids):
        started = []
        for place, first, width, halo, halo_first in spec["pieces"]:
            for half in range(2):
                lanes = pl.ds(128 * half, 128)
                cols = pl.ds(place, width)
                for source, begin, target in (
                    (own, first, grid.at[:, pl.ds(0, rows), half, cols, :]),
                    (refs[2 + halo], halo_first, grid.at[:, pl.ds(rows, MARGIN), half, cols, :]),
                ):
                    copy = pltpu.make_async_copy(
                        source.at[:, :, pl.ds(begin, width), lanes],
                        target,
                        sems.at[sum(map(len, copies)) + len(started)],
                    )
                    copy.start()
                    started.append(copy)
        copies.append(started)
    lat_shift = offsets[0]
    lon_shift = offsets[1]
    for spec, grid, out_ref, started in zip(specs, grids, outs, copies):
        for copy in started:
            copy.wait()
        for column in range(spec["count"]):
            start = spec["start"] + column * WLON + lon_shift
            for step in range(rows // WLAT):
                for level in range(LEVELS):
                    for row in range(WLAT):
                        token = step * SPAN + (level * WLAT + row) * WLON
                        for half in range(2):
                            lanes = slice(128 * half, 128 * half + 128)
                            out_ref[column, pl.ds(token, WLON), lanes] = grid[
                                level,
                                lat_shift + step * WLAT + row,
                                half,
                                pl.ds(start, WLON),
                                :,
                            ]


def roll_in(offsets, grid, halos, parts, after):
    rows, cols, features = grid.shape[1:]
    used, specs, scratch, out_shape = [], [], [], []
    for begin, end in parts:
        low = (begin * WLON + 1) // 8 * 8
        high = (end * WLON + WLON - 2) // 8 * 8 + 8
        pieces = []
        for wrap in range(2):
            for first, array in halos:
                left = max(low - wrap * cols, first)
                right = min(high - wrap * cols, first + array.shape[2])
                if left < right:
                    place = left + wrap * cols - low
                    pieces.append((place, left, right - left, len(used), left - first))
                    used.append(array)
        specs.append(dict(pieces=pieces, start=begin * WLON - low, count=end - begin))
        scratch.append(VMEM((LEVELS, rows + MARGIN, 2, high - low, 128), F32))
        shape = (end - begin, rows // WLAT * SPAN, features)
        out_shape.append(jax.ShapeDtypeStruct(shape, F32))
    count = 4 * sum(len(spec["pieces"]) for spec in specs)
    return pl.pallas_call(
        functools.partial(roll_kernel, specs, rows),
        out_shape=out_shape,
        in_specs=[SMEM] + [ANYWHERE] * (1 + len(used) + len(after)),
        out_specs=[WHOLE] * len(parts),
        scratch_shapes=scratch + [pltpu.SemaphoreType.DMA((count,))],
        compiler_params=pltpu.CompilerParams(vmem_limit_bytes=LIMIT),
        cost_estimate=SMALL,
        name="roll_in",
    )(offsets, in_hbm(grid), *used, *after)


def margin_kernel(near, low, cols, first_ref, second_ref, *refs):
    near_ref, far_ref, sems = refs[-3:]
    copies = []
    for index, source in enumerate((first_ref, second_ref)):
        for begin, width, target, place in (
            (0, near, near_ref, 0),
            (low, cols - low, far_ref, 0),
            (0, 16, far_ref, cols - low),
        ):
            copy = pltpu.make_async_copy(
                source.at[:, pl.ds(0, MARGIN), pl.ds(begin, width), :],
                target.at[index, :, :, pl.ds(place, width), :],
                sems.at[len(copies)],
            )
            copy.start()
            copies.append(copy)
    for copy in copies:
        copy.wait()


def margins_of(first, second, near, low, after):
    levels, _, cols, features = first.shape
    return pl.pallas_call(
        functools.partial(margin_kernel, near, low, cols),
        out_shape=[
            jax.ShapeDtypeStruct((2, levels, MARGIN, near, features), F32),
            jax.ShapeDtypeStruct((2, levels, MARGIN, cols - low + 16, features), F32),
        ],
        in_specs=[ANYWHERE] * (2 + len(after)),
        out_specs=[WHOLE] * 2,
        scratch_shapes=[pltpu.SemaphoreType.DMA((6,))],
        compiler_params=pltpu.CompilerParams(vmem_limit_bytes=LIMIT),
        cost_estimate=SMALL,
        name="margins",
    )(in_hbm(first), in_hbm(second), *after)


def unroll_kernel(spec, rows, *refs):
    offsets = refs[0]
    count = spec["count"]
    own = refs[1 : 1 + count]
    tail = refs[1 + count : 1 + 2 * count]
    if spec["targets"]:
        out_hbm, grid, out_ref, sems = refs[-4:]
    else:
        out_ref, grid = refs[-2:]
    lat_shift = offsets[0]
    lon_shift = offsets[1]
    for column in range(count):
        for level in range(LEVELS):
            for row in range(WLAT):
                token = (level * WLAT + row) * WLON
                for half in range(2):
                    lanes = slice(128 * half, 128 * half + 128)
                    cols = pl.ds(column * WLON, WLON)
                    grid[level, row, half, cols, :] = tail[column][0, pl.ds(token, WLON), lanes]
                    for step in range(rows // WLAT):
                        grid[level, WLAT + step * WLAT + row, half, cols, :] = own[column][
                            0, pl.ds(step * SPAN + token, WLON), lanes
                        ]
    start = spec["start"] - lon_shift
    width = spec["width"]
    copies = []
    for level in range(LEVELS):
        for row in range(rows):
            for half in range(2):
                out_ref[level, row, :, 128 * half : 128 * half + 128] = grid[
                    level, WLAT + row - lat_shift, half, pl.ds(start, width), :
                ]
        for place, first, size in spec["targets"]:
            copy = pltpu.make_async_copy(
                out_ref.at[level, :, pl.ds(place, size), :],
                out_hbm.at[level, :, pl.ds(first, size), :],
                sems.at[len(copies)],
            )
            copy.start()
            copies.append(copy)
    for copy in copies:
        copy.wait()


def targets_of(start, end, cols):
    edge = min(end, cols)
    return [(0, start, edge - start)] + ([(cols - start, 0, end - cols)] if end > cols else [])


def roll_back(offsets, own, tail, first, start, end, shape, after, into=()):
    count = len(own)
    levels, rows, cols, features = shape
    tokens = own[0][0].shape[1]
    width = end - start
    spec = dict(count=count, start=start - first, width=width)
    spec["targets"] = targets_of(start, end, cols) if into else []

    def spec_of(entry, tall):
        index, lane = (entry[1:] + (0,))[:2]
        return pl.BlockSpec((1, tall, features), lambda i: (index, 0, lane))

    scratch = [VMEM((levels, rows + WLAT, 2, count * WLON + 16, 128), F32)]
    piece = (levels, rows, width, features)
    base = [array for array in into if array is not None]
    if into:
        out_shape, out_spec = shape, ANYWHERE
        scratch += [VMEM(piece, F32), pltpu.SemaphoreType.DMA((2 * levels,))]
    else:
        out_shape, out_spec = piece, pl.BlockSpec(piece, lambda i: (0, 0, 0, 0))
    return pl.pallas_call(
        functools.partial(unroll_kernel, spec, rows),
        out_shape=(pltpu.HBM if into else jax.ShapeDtypeStruct)(out_shape, F32),
        grid=(1,),
        in_specs=[SMEM]
        + [spec_of(entry, tokens) for entry in own]
        + [spec_of(entry, SPAN) for entry in tail]
        + [ANYWHERE] * (len(base) + len(after)),
        out_specs=out_spec,
        scratch_shapes=scratch,
        input_output_aliases={1 + 2 * count: 0} if base else {},
        compiler_params=pltpu.CompilerParams(vmem_limit_bytes=LIMIT),
        cost_estimate=SMALL,
        name="roll_back",
    )(
        offsets,
        *[in_hbm(entry[0]) for entry in own],
        *[entry[0] for entry in tail],
        *[in_hbm(array) for array in base],
        *after,
    )


def place_kernel(targets, piece_hbm, *refs):
    out_hbm, held, sems = refs[-3:]
    inward, outward = [], []
    for level in range(LEVELS):
        copy = pltpu.make_async_copy(piece_hbm.at[level], held.at[level], sems.at[level])
        copy.start()
        inward.append(copy)
    for level in range(LEVELS):
        inward[level].wait()
        for place, first, size in targets:
            copy = pltpu.make_async_copy(
                held.at[level, :, pl.ds(place, size), :],
                out_hbm.at[level, :, pl.ds(first, size), :],
                sems.at[LEVELS + len(outward)],
            )
            copy.start()
            outward.append(copy)
    for copy in outward:
        copy.wait()


def placed_in(grid, piece, start, shape, after):
    targets = targets_of(start, start + piece.shape[2], shape[2])
    base = [] if grid is None else [grid]
    return pl.pallas_call(
        functools.partial(place_kernel, targets),
        out_shape=pltpu.HBM(shape, F32),
        in_specs=[ANYWHERE] * (1 + len(base) + len(after)),
        out_specs=ANYWHERE,
        scratch_shapes=[VMEM(piece.shape, F32), pltpu.SemaphoreType.DMA((3 * LEVELS,))],
        input_output_aliases={1: 0} if base else {},
        compiler_params=pltpu.CompilerParams(vmem_limit_bytes=LIMIT),
        cost_estimate=SMALL,
        name="place",
    )(piece, *[in_hbm(array) for array in base], *after)


def row_sums(value):
    return jnp.sum(value.reshape(value.shape[0] // 8, 8, value.shape[1]), axis=0)


def block_kernel(
    begin,
    halo_first,
    given,
    waits,
    offsets,
    recv_ref,
    earlier_hbm,
    cot_hbm,
    halo_hbm,
    live_ref,
    mod_ref,
    w_qkv_ref,
    w_qkv_t_ref,
    bias_ref,
    w_out_ref,
    w_out_t_ref,
    vec_ref,
    w_up_ref,
    w_up_t_ref,
    b_up_ref,
    w_down_ref,
    w_down_t_ref,
    *refs,
):
    (
        res_ref,
        grad_ref,
        tail_ref,
        acc_main,
        acc_bias,
        acc_small,
        fetched,
        sems,
        x_s,
        g_s,
        normed_s,
        inv_s,
        ln_in_s,
        proj_s,
        prob_s,
        prob_low_s,
        q_wide_s,
        d_wide_s,
        dscore_s,
        q_wide_t,
        d_wide_t,
        att_t,
        dq_t,
        ln_two_s,
        act_s,
        dhid_s,
        branch_s,
        attg_s,
        gproj_s,
        att_s,
        gatt_s,
        normed_two_s,
        inv_two_s,
        first_s,
        pre_s,
        back_s,
        turned_one,
        turned_two,
    ) = refs[given + waits :]
    width = recv_ref.shape[-1]
    tokens = recv_ref.shape[1]
    count = tokens // SPAN
    hidden = w_up_ref.shape[1]
    head_size = width // HEADS
    wide = HEADS * SPAN
    scale = head_size ** (-0.5)

    @pl.when(pl.program_id(0) == 0)
    def _():
        for index, target in enumerate((acc_main, acc_bias, acc_small)):
            target[...] = refs[index][...] if given else jnp.zeros_like(target)

    step = pl.program_id(0)
    grid_rows = earlier_hbm.shape[1]
    grid_cols = earlier_hbm.shape[2]
    lat_shift = offsets[0]
    lon_shift = offsets[1]

    def place_of(at):
        first = (begin + at) * WLON + lon_shift
        return first // 8 * 8, first % 8

    def copies_of(at, slot):
        first, _ = place_of(at)
        whole, split = [], []
        for index, source in enumerate((earlier_hbm, cot_hbm)):
            for half in range(2):
                lanes = pl.ds(128 * half, 128)
                own = fetched.at[slot, index, :, pl.ds(0, grid_rows), half]
                sem = sems.at[slot, 4 * index + 2 * half]
                cols = pl.ds(pl.multiple_of(first, 8), REACH)
                whole.append((source.at[:, :, cols, lanes], own, sem))
                for j in range(0, REACH, 8):
                    cols = pl.ds(pl.multiple_of((first + j) % grid_cols, 8), 8)
                    split.append((source.at[:, :, cols, lanes], own.at[:, :, pl.ds(j, 8), :], sem))
        return whole, split

    def halo_copies_of(at, slot):
        first, _ = place_of(at)
        cols = pl.ds(pl.multiple_of(first - halo_first, 8), REACH)
        copies = []
        for index in range(2):
            for half in range(2):
                copies.append(
                    (
                        halo_hbm.at[index, :, :, cols, pl.ds(128 * half, 128)],
                        fetched.at[slot, index, :, pl.ds(grid_rows, MARGIN), half],
                        sems.at[slot, 4 * index + 2 * half + 1],
                    )
                )
        return copies

    def fetch(at, slot):
        first, _ = place_of(at)
        whole, split = copies_of(at, slot)

        @pl.when(first + REACH <= grid_cols)
        def _():
            for copy in whole:
                pltpu.make_async_copy(*copy).start()

        @pl.when(first + REACH > grid_cols)
        def _():
            for copy in split:
                pltpu.make_async_copy(*copy).start()

        for copy in halo_copies_of(at, slot):
            pltpu.make_async_copy(*copy).start()

    slot = step % 2

    @pl.when(step == 0)
    def _():
        fetch(0, 0)

    @pl.when(step + 1 < pl.num_programs(0))
    def _():
        fetch(step + 1, 1 - slot)

    for source, target, sem in copies_of(0, slot)[0] + halo_copies_of(0, slot):
        pltpu.make_async_copy(source, target, sem).wait()
    _, inside = place_of(step)
    for index, target in enumerate((x_s, g_s)):
        for part in range(count):
            for level in range(LEVELS):
                for row in range(WLAT):
                    token = part * SPAN + (level * WLAT + row) * WLON
                    for half in range(2):
                        target[pl.ds(token, WLON), 128 * half : 128 * half + 128] = fetched[
                            slot, index, level, lat_shift + part * WLAT + row, half, pl.ds(inside, WLON), :
                        ]

    shift_one = mod_ref[0:1, :]
    gain_one = mod_ref[1:2, :]
    b_out = vec_ref[0:1, :]
    gain_two = vec_ref[1:2, :]
    bias_two = vec_ref[2:3, :]
    b_down = vec_ref[3:4, :]

    group = 128 // head_size
    groups = [
        (slice(first * TILE, (first + group) * TILE), slice(first * head_size, first * head_size + 128))
        for first in range(0, HEADS, group)
    ]
    rest = slice(HEADS * TILE, wide)

    @pl.when(step == 0)
    def _():
        for part in range(count):
            for lanes, own in groups + [(rest, slice(0, width))]:
                for target in (q_wide_s, d_wide_s):
                    target[part, lanes, own] = jnp.zeros_like(target[part, lanes, own])
                for target in (q_wide_t, d_wide_t):
                    target[part, own, lanes] = jnp.zeros_like(target[part, own, lanes])

    def spread_heads(value, turned, target, target_t):
        for head in range(HEADS):
            own = slice(head * head_size, (head + 1) * head_size)
            tile = pl.ds(head * TILE, TILE)
            rest = pl.ds(HEADS * TILE + head * REST, REST)
            target[tile, own] = value[:TILE, own]
            target[rest, own] = value[TILE:, own]
            target_t[own, tile] = turned[own, :TILE]
            target_t[own, rest] = turned[own, TILE:]

    def head_products(turned, scores, target):
        last = dot_nn(turned, scores[:, pl.ds(HEADS * TILE, HEADS * REST)])
        for head in range(HEADS):
            own = slice(head * head_size, (head + 1) * head_size)
            first = dot_nn(turned[own, :], scores[:, pl.ds(head * TILE, TILE)])
            target[own, 0:TILE] = first.astype(BF16)
            target[own, TILE:SPAN] = last[own, head * REST : (head + 1) * REST].astype(BF16)

    def wide_product(left, wide_t, start, size):
        features = slice(0, width)
        if start < rest.start:
            features = groups[start // (group * TILE)][1]
        return dot_nn(left[:, features], wide_t[features, start : start + size])

    def wide_sum(scores, wide_s):
        parts = [dot_nn(scores[:, lanes], wide_s[lanes, own]) for lanes, own in groups]
        return jnp.concatenate(parts, axis=1) + dot_nn(scores[:, rest], wide_s[rest, :])

    everything = count * SPAN
    blocks = [slice(start, start + BLOCK) for start in range(0, everything, BLOCK)]
    items = [
        (part, start, min(WIDE, wide - start))
        for part in range(count)
        for start in range(0, wide, WIDE)
    ]

    def rows_of(part):
        return slice(part * SPAN, (part + 1) * SPAN)

    def ahead(products, work):
        held = products[0]()
        for index in range(len(products)):
            later = products[index + 1]() if index + 1 < len(products) else None
            work(index, held)
            held = later

    def normalized(value):
        centered = value - jnp.mean(value, axis=-1, keepdims=True)
        inv = lax.rsqrt(jnp.mean(centered * centered, axis=-1, keepdims=True) + EPS)
        return centered * inv, inv

    def norm_back(hat, normed, inv):
        first = jnp.mean(hat, axis=-1, keepdims=True)
        second = jnp.mean(hat * normed, axis=-1, keepdims=True)
        return inv * (hat - first - normed * second)

    def add_small(place, values):
        acc_small[:, place * width : (place + 1) * width] += functools.reduce(jnp.add, values)

    for rows in blocks:
        x = recv_ref[0, rows, :] + x_s[rows, :]
        x_s[rows, :] = x
        normed, inv = normalized(x)
        normed_s[rows, :] = normed
        inv_s[rows, :] = inv
        ln_in_s[rows, :] = (normed * gain_one + shift_one).astype(BF16)
    for start in range(0, 3 * width, WIDE):
        lanes = slice(start, min(start + WIDE, 3 * width))
        proj_s[:, lanes] = dot_nn(ln_in_s[...], w_qkv_ref[:, lanes]).astype(BF16)

    live = []
    for part in range(count):
        rows = rows_of(part)
        live.append(jnp.broadcast_to(live_ref[0, rows, :], (SPAN, 128)))
        queries = proj_s[rows, 0:width]
        spread_heads(queries, queries.T, q_wide_s.at[part], q_wide_t.at[part])

    def raw_scores(item):
        part, start, size = item
        keys = proj_s[rows_of(part), width : 2 * width]
        return wide_product(keys, q_wide_t.at[part], start, size)

    def softmax(index, raw):
        part, start, size = items[index]
        for place in range(0, size, 128):
            lanes = slice(start + place, start + place + 128)
            scores = raw[:, place : place + 128] * (scale * LOG2E) + bias_ref[:, lanes]
            scores = jnp.where(live[part] > 0.5, scores, NEG)
            expo = jnp.exp2(scores - jnp.max(scores, axis=0, keepdims=True))
            prob = expo * (1.0 / jnp.sum(expo, axis=0, keepdims=True))
            prob_s[part, :, lanes] = prob
            prob_low_s[part, :, lanes] = prob.astype(BF16)
        if start + size == wide:
            values_t = proj_s[rows_of(part), 2 * width : 3 * width].T
            head_products(values_t, prob_low_s.at[part], att_t.at[part])

    ahead([functools.partial(raw_scores, item) for item in items], softmax)

    for part in range(count):
        att_s[rows_of(part), :] = att_t[part].T
    first_s[...] = dot_nn(att_s[...], w_out_ref[...])
    for rows in blocks:
        mid = x_s[rows, :] + first_s[rows, :] + b_out
        x_s[rows, :] = mid
        normed, inv = normalized(mid)
        normed_two_s[rows, :] = normed
        inv_two_s[rows, :] = inv
        ln_two_s[rows, :] = (normed * gain_two + bias_two).astype(BF16)
        branch_s[rows, :] = g_s[rows, :].astype(BF16)

    def feed(start):
        lanes = slice(start, start + WIDE)
        slot = start // WIDE % 2
        pre_s[slot] = dot_nn(ln_two_s[...], w_up_ref[:, lanes])
        back_s[slot] = dot_nn(branch_s[...], w_down_t_ref[:, lanes])

    def gelu(index, _):
        for first in range(0, WIDE, width):
            gelu_part(index * WIDE + first, index % 2, slice(first, first + width))

    def gelu_part(start, slot, inside):
        lanes = slice(start, start + width)
        sums = []
        for rows in blocks:
            pre = pre_s[slot, rows, inside] + b_up_ref[:, lanes]
            square = pre * pre
            half = 0.5 + 0.5 * jnp.tanh(pre * (GELU_ONE + GELU_TWO * square))
            act_s[rows, lanes] = (pre * half).astype(BF16)
            slope = pre * (2 * GELU_ONE + (6 * GELU_TWO) * square)
            dhid = back_s[slot, rows, inside] * (half * (1.0 + (1.0 - half) * slope))
            dhid = dhid.astype(BF16)
            dhid_s[rows, lanes] = dhid
            sums.append(row_sums(dhid.astype(F32)))
        add_small(6 + start // width, sums)

    ahead([functools.partial(feed, start) for start in range(0, hidden, WIDE)], gelu)

    first_s[...] = dot_nn(dhid_s[...], w_up_t_ref[...])
    res_ref[0] = dot_nn(act_s[...], w_down_ref[...])
    sums = [[], [], [], []]
    for rows in blocks:
        g_ln = first_s[rows, :]
        normed = normed_two_s[rows, :]
        grad_mid = g_s[rows, :] + norm_back(g_ln * gain_two, normed, inv_two_s[rows, :])
        grad_ref[0, rows, :] = grad_mid
        att_grad = grad_mid.astype(BF16)
        attg_s[rows, :] = att_grad
        for place, value in enumerate(
            (branch_s[rows, :].astype(F32), g_ln * normed, g_ln, att_grad.astype(F32))
        ):
            sums[place].append(row_sums(value))
    for place in range(4):
        add_small(place, sums[place])

    gatt_s[...] = dot_nn(attg_s[...], w_out_t_ref[...]).astype(BF16)
    for rows in blocks:
        result = res_ref[0, rows, :] + x_s[rows, :] + b_down
        res_ref[0, rows, :] = result
        if rows.start >= (count - 1) * SPAN:
            start = rows.start - (count - 1) * SPAN
            tail_ref[0, start : start + BLOCK, 0:width] = result
    for part in range(count):
        g_att = gatt_s[rows_of(part), :]
        spread_heads(g_att, g_att.T, d_wide_s.at[part], d_wide_t.at[part])

    def add_main(place, total):
        acc_main[place * width : (place + 1) * width, :] += total

    def out_gradient():
        total = dot_nn(att_t[0], attg_s[rows_of(0), :])
        for part in range(1, count):
            total += dot_nn(att_t[part], attg_s[rows_of(part), :])
        add_main(3, total)

    def feed_gradient(place, left, right, start):
        total = dot_nn(left[...], right[:, start : start + WIDE])
        for first in range(0, total.shape[1], width):
            add_main(place + first // width, total[:, first : first + width])

    turned_one[...] = ln_two_s[...].T
    turned_two[...] = branch_s[...].T
    extra = [out_gradient]
    for start in range(0, hidden, WIDE):
        place = 4 + start // width
        extra.append(functools.partial(feed_gradient, place, turned_one, dhid_s, start))
    for start in range(0, hidden, WIDE):
        place = 4 + (hidden + start) // width
        extra.append(functools.partial(feed_gradient, place, turned_two, act_s, start))

    def d_probs(item):
        part, start, size = item
        values = proj_s[rows_of(part), 2 * width : 3 * width]
        return wide_product(values, d_wide_t.at[part], start, size)

    def d_scores(index, d_prob):
        part, start, size = items[index]
        rows = rows_of(part)
        if extra:
            extra.pop(0)()
        for place in range(0, size, 128):
            lanes = slice(start + place, start + place + 128)
            own = d_prob[:, place : place + 128]
            prob = prob_s[part, :, lanes]
            inside = jnp.sum(own * prob, axis=0, keepdims=True)
            d_score = prob * (own - inside)
            acc_bias[:, lanes] += d_score
            dscore_s[part, :, lanes] = (d_score * scale).astype(BF16)
        if start + size == wide:
            d_values = wide_sum(prob_low_s.at[part], d_wide_s.at[part])
            d_keys = wide_sum(dscore_s.at[part], q_wide_s.at[part])
            keys_t = proj_s[rows, width : 2 * width].T
            head_products(keys_t, dscore_s.at[part], dq_t.at[part])
            gproj_s[rows, 0:width] = dq_t[part].T
            gproj_s[rows, width : 2 * width] = d_keys.astype(BF16)
            gproj_s[rows, 2 * width : 3 * width] = d_values.astype(BF16)

    ahead([functools.partial(d_probs, item) for item in items], d_scores)
    for rest in extra:
        rest()

    first_s[...] = dot_nn(gproj_s[...], w_qkv_t_ref[...])
    turned_one[...] = ln_in_s[...].T
    for start in range(0, 3 * width, WIDE):
        feed_gradient(start // width, turned_one, gproj_s, start)
    sums = [[], []]
    for rows in blocks:
        g_ln = first_s[rows, :]
        normed = normed_s[rows, :]
        total = grad_ref[0, rows, :] + norm_back(g_ln * gain_one, normed, inv_s[rows, :])
        grad_ref[0, rows, :] = total
        if rows.start >= (count - 1) * SPAN:
            start = rows.start - (count - 1) * SPAN
            tail_ref[0, start : start + BLOCK, width : 2 * width] = total
        sums[0].append(row_sums(g_ln))
        sums[1].append(row_sums(g_ln * normed))
    for place in range(2):
        add_small(4 + place, sums[place])


def run_block(
    offsets, begin, received, earlier, cot, halo, halo_first, live, fixed, sums, sum_shapes, after
):
    columns, tall, width = received.shape
    count = tall // SPAN
    hidden = fixed[7].shape[1]
    wide = HEADS * SPAN
    rows = earlier.shape[1]

    def moving(tall_size, last, first=0):
        return pl.BlockSpec((1, tall_size, last), lambda i: (i + first, 0, 0))

    def still(array):
        place = (0,) * len(array.shape)
        return pl.BlockSpec(array.shape, lambda i: place, pipeline_mode=pl.Buffered(1))

    in_specs = [SMEM, moving(tall, width)] + [ANYWHERE] * 3 + [moving(tall, 1, begin)]
    first_sum = len(in_specs) + len(fixed)
    in_specs += [still(array) for array in fixed] + [still(array) for array in sums]
    in_specs += [ANYWHERE] * len(after)
    shapes = [pltpu.HBM(sum_shapes[0], F32)]
    shapes += [jax.ShapeDtypeStruct(shape, F32) for shape in sum_shapes[1:]]
    out_specs = [moving(tall, width)] * 2 + [moving(SPAN, 2 * width)] + [still(a) for a in shapes]
    out_shape = (
        [pltpu.HBM((columns, tall, width), F32)] * 2
        + [jax.ShapeDtypeStruct((columns, SPAN, 2 * width), F32)]
        + shapes
    )
    return pl.pallas_call(
        functools.partial(block_kernel, begin, halo_first, len(sums), len(after)),
        out_shape=out_shape,
        grid=(columns,),
        in_specs=in_specs,
        out_specs=out_specs,
        scratch_shapes=[
            VMEM((2, 2, LEVELS, rows + MARGIN, 2, 24, 128), F32),
            pltpu.SemaphoreType.DMA((2, 8)),
            VMEM((tall, width), F32),
            VMEM((tall, width), F32),
            VMEM((tall, width), F32),
            VMEM((tall, 1), F32),
            VMEM((tall, width), BF16),
            VMEM((tall, 3 * width), BF16),
            VMEM((count, SPAN, wide), F32),
            VMEM((count, SPAN, wide), BF16),
            VMEM((count, wide, width), BF16),
            VMEM((count, wide, width), BF16),
            VMEM((count, SPAN, wide), BF16),
            VMEM((count, width, wide), BF16),
            VMEM((count, width, wide), BF16),
            VMEM((count, width, SPAN), BF16),
            VMEM((count, width, SPAN), BF16),
            VMEM((tall, width), BF16),
            VMEM((tall, hidden), BF16),
            VMEM((tall, hidden), BF16),
            VMEM((tall, width), BF16),
            VMEM((tall, width), BF16),
            VMEM((tall, 3 * width), BF16),
            VMEM((tall, width), BF16),
            VMEM((tall, width), BF16),
            VMEM((tall, width), F32),
            VMEM((tall, 1), F32),
            VMEM((tall, width), F32),
            VMEM((2, tall, WIDE), F32),
            VMEM((2, tall, WIDE), F32),
            VMEM((width, tall), BF16),
            VMEM((width, tall), BF16),
        ],
        input_output_aliases={first_sum + i: 3 + i for i in range(len(sums))},
        compiler_params=pltpu.CompilerParams(vmem_limit_bytes=BLOCK_LIMIT),
        cost_estimate=pl.CostEstimate(
            flops=columns * 10**10, bytes_accessed=1, transcendentals=0
        ),
        name="block",
    )(offsets, received, in_hbm(earlier), in_hbm(cot), halo, live, *fixed, *sums, *after)


def window_tokens(grid):
    shape = grid.shape
    blocks = grid.reshape((shape[0], shape[1] // WLAT, WLAT, shape[2] // WLON, WLON))
    return blocks.transpose((3, 1, 0, 2, 4)).reshape((shape[2] // WLON, -1, 1))


SHARES = (4, 4, 4, 4)


def on_device(
    state,
    earlier,
    cotangent,
    level_mask,
    window_offsets,
    lead_index,
    embeddings,
    w_mod,
    b_mod,
    w_qkv,
    bias_table,
    w_out,
    b_out,
    norm_gain,
    norm_bias,
    w_up,
    b_up,
    w_down,
    b_down,
):
    width = state.shape[-1]
    rows = state.shape[2]
    cols = state.shape[3]
    hidden = w_up.shape[1]
    total = cols // WLON
    offsets = window_offsets[0]
    lat_shift = offsets[0]
    lon_shift = offsets[1]
    ends = [int(total * share) // sum(SHARES) for share in np.cumsum(SHARES)]
    steps = list(zip([0] + ends[:-1], ends))
    near = ((ends[0] - 1) * WLON + WLON - 1) // 8 * 8 + REACH
    far = (ends[0] * WLON + 1) // 8 * 8

    next_offsets = passed_along(offsets, "lead", -1)
    state_halos = [
        (low, passed_along(state[0][:, :MARGIN, low:high], "lat", -1))
        for low, high in ((0, near), (near, cols))
    ]
    grid_live = level_mask[0].astype(F32)
    live_halo = passed_along(grid_live[:, :MARGIN], "lat", -1)
    moved = []
    for step in steps:
        moved += roll_in(next_offsets, state[0], state_halos, [step], moved[-1:] or [live_halo])
    received = [passed_along(array, "lead", 1) for array in moved]
    margins = margins_of(earlier[0], cotangent[0], near, far, moved[:1])
    halos = [passed_along(margin, "lat", -1) for margin in margins]

    extended = jnp.concatenate([grid_live, live_halo], axis=1)
    shifted = lax.dynamic_slice_in_dim(extended, lat_shift, rows, 1)
    doubled = jnp.concatenate([shifted, shifted], axis=2)
    live = window_tokens(lax.dynamic_slice_in_dim(doubled, lon_shift, cols, 2))

    emb_row = lax.dynamic_index_in_dim(embeddings, lead_index[0], 0, keepdims=False)
    modulation = jnp.dot(emb_row, w_mod, precision=HIGH) + b_mod
    mod = jnp.stack([modulation[:width], 1.0 + modulation[width:]])
    vectors = jnp.stack([b_out, norm_gain, norm_bias, b_down])
    bias, w_qkv_t, w_out_t, w_up_t, w_down_t = prepare(
        bias_table, [w_qkv, w_out, w_up, w_down], moved[1:2]
    )
    fixed = [
        mod,
        w_qkv,
        w_qkv_t,
        bias,
        w_out,
        w_out_t,
        vectors,
        w_up,
        w_up_t,
        b_up[None],
        w_down,
        w_down_t,
    ]
    main_rows = 4 * width + 2 * hidden
    few = 6 * width + hidden
    table_rows = HEADS * TABLE_PAD // width
    mod_rows = 2 * embeddings.shape[0]
    used = main_rows + few // width + table_rows + mod_rows
    unit = 8 * lax.axis_size("lat") * lax.axis_size("lead")
    buffer_rows = -(-used // unit) * unit
    sum_shapes = [(buffer_rows, width), (SPAN, HEADS * SPAN), (8, few)]
    sums = []

    results, grads = [], []
    shape = earlier.shape[1:]

    def back(kept, start, end, after, into=()):
        low = (start - (WLON - 1)) // WLON
        high = (end - 2) // WLON
        picked = [kept[window % total] for window in range(low, high + 1)]
        own, tail = zip(*picked)
        return roll_back(offsets, own, tail, low * WLON, start, end, shape, after, into)

    bounds = [(end * WLON + 1) // 16 * 16 for end in ends[:-1]] + [cols + 16]
    pieces = list(zip([16] + bounds[:-1], bounds))
    rolled, grad_pieces = [], []
    for index, (begin, end) in enumerate(steps):
        made = run_block(
            offsets,
            begin,
            received[index],
            earlier[0],
            cotangent[0],
            halos[min(index, 1)],
            0 if index == 0 else far,
            live,
            fixed,
            sums,
            sum_shapes,
            moved[1:2] if index == 0 else rolled[-1:],
        )
        sums = made[3:]
        tail = passed_along(made[2], "lat", 1)
        for window in range(begin, end):
            results.append(((made[0], window - begin), (tail, window - begin, 0)))
            grads.append(((made[1], window - begin), (tail, window - begin, 1)))
        if index == len(steps) - 2:
            rolled.append(back(grads, pieces[0][0], pieces[index - 1][1], [made[4]]))
            grad_pieces.append(passed_along(rolled[-1], "lead", -1))
    rolled.append(back(grads, *pieces[-2], [made[4]]))
    grad_pieces.append(passed_along(rolled[-1], "lead", -1))
    buffer = collect(lead_index, embeddings.shape[0], sums[1], sums[2], sums[0], main_rows, rolled[-1:])
    part = scattered_sum(buffer, [])
    rolled.append(back(grads, *pieces[-1], [part] + grad_pieces))
    grad_pieces.append(passed_along(rolled[-1], "lead", -1))
    block_out = back(results, pieces[0][0], pieces[-3][1], rolled[-1:], (None,))
    block_out = back(results, pieces[-2][0], pieces[-1][1], [], (block_out,))
    state_grad = placed_in(None, grad_pieces[0], pieces[0][0], shape, [in_hbm(block_out)])
    state_grad = placed_in(state_grad, grad_pieces[1], pieces[-2][0], shape, [])
    own, others = gathered(part, [in_hbm(state_grad)])
    state_grad = placed_in(state_grad, grad_pieces[2], pieces[-1][0], shape, [])
    outs = finished(own, others, embeddings, width, hidden)
    return (block_out[None], state_grad[None]) + outs


def solution(mesh):
    grid = P("lead", None, "lat", None, None)
    placed = (grid, grid, grid, P("lead", None, "lat", None), P("lead", None), P("lead"))
    return jax.shard_map(
        on_device,
        mesh=mesh,
        in_specs=placed + (P(),) * 13,
        out_specs=(grid, grid) + (P(),) * 12,
        check_vma=False,
    )
```

```python
import functools

import jax
import jax.numpy as jnp
import numpy as np
from jax import lax
from jax.experimental import pallas as pl
from jax.experimental.pallas import tpu as pltpu
from jax.sharding import PartitionSpec as P

HEADS = 8
LEVELS = 2
WLAT = 6
WLON = 12
SPAN = LEVELS * WLAT * WLON
MARGIN = WLAT - 1
SPAN_ROW = 2 * WLAT - 1
SPAN_COL = 2 * WLON - 1
TABLE_ROWS = (2 * LEVELS - 1) * SPAN_ROW * SPAN_COL
TABLE_PAD = 768
TILE = 128
REST = SPAN - TILE
LOG2E = 1.4426950408889634
GELU_ONE = 0.7978845608028654
GELU_TWO = GELU_ONE * 0.044715
REACH = 24
BLOCK = 48
WIDE = 512

EPS = 1e-06
NEG = -1000000000.0
HIGH = lax.Precision.HIGHEST
F32 = jnp.float32
BF16 = jnp.bfloat16
VMEM = pltpu.VMEM
WHOLE = pl.BlockSpec(memory_space=pltpu.VMEM)
SMEM = pl.BlockSpec(memory_space=pltpu.SMEM)
ANYWHERE = pl.BlockSpec(memory_space=pl.ANY)
SMALL = pl.CostEstimate(flops=1, bytes_accessed=1, transcendentals=0)
LIMIT = 30 * 1024 * 1024
BLOCK_LIMIT = 62 * 1024 * 1024


def passed_along(value, axis, steps):
    count = lax.axis_size(axis)
    pairs = [(source, (source + steps) % count) for source in range(count)]
    return lax.ppermute(value, axis, pairs)


def in_hbm(array):
    return pltpu.with_memory_space_constraint(array, pltpu.HBM)


def dot_nn(a, b):
    return lax.dot_general(a, b, (((1,), (0,)), ((), ())), preferred_element_type=F32)


def prepare_kernel(count, table_ref, *refs):
    out_ref, scratch = refs[-count - 2], refs[-1]
    for source, target in zip(refs[:count], refs[-count - 1 : -1]):
        target[...] = source[...].T
    table = table_ref[...]
    lanes = lax.broadcasted_iota(jnp.int32, (384, SPAN), 0)
    cell = lax.broadcasted_iota(jnp.int32, (384, SPAN), 1)
    place = (
        (cell // (WLAT * WLON)) * (SPAN_ROW * SPAN_COL)
        + ((cell // WLON) % WLAT) * SPAN_COL
        + cell % WLON
    )
    pick = (lanes == place).astype(F32)
    base = (SPAN_ROW * SPAN_COL) * (LEVELS - 1) + SPAN_COL * (WLAT - 1) + WLON - 1
    for group in range(LEVELS * WLAT):
        level, row = divmod(group, WLAT)
        start = level * SPAN_ROW * SPAN_COL + row * SPAN_COL - group * WLON - base
        moved = pltpu.roll(table, start % TABLE_PAD, 1)
        for head in range(HEADS):
            scratch[head, pl.ds(group * WLON, WLON), :] = jnp.broadcast_to(
                moved[head : head + 1], (WLON, TABLE_PAD)
            )
    for head in range(HEADS):
        rows = pltpu.roll(scratch[head], 0, 1, stride=1, stride_axis=0)
        values = jnp.dot(rows[:, :384], pick, precision=HIGH, preferred_element_type=F32) * LOG2E
        out_ref[:, pl.ds(head * TILE, TILE)] = values[:, :TILE]
        out_ref[:, pl.ds(HEADS * TILE + head * REST, REST)] = values[:, TILE:]


def prepare(bias_table, weights, after):
    padded = jnp.pad(bias_table, ((0, 0), (0, TABLE_PAD - TABLE_ROWS)))
    return pl.pallas_call(
        functools.partial(prepare_kernel, len(weights)),
        out_shape=[pltpu.HBM((SPAN, HEADS * SPAN), F32)]
        + [pltpu.HBM(array.shape[::-1], array.dtype) for array in weights],
        in_specs=[WHOLE] * (1 + len(weights)) + [ANYWHERE] * len(after),
        out_specs=[WHOLE] * (1 + len(weights)),
        scratch_shapes=[VMEM((HEADS, SPAN, TABLE_PAD), F32)],
        compiler_params=pltpu.CompilerParams(vmem_limit_bytes=LIMIT),
        cost_estimate=SMALL,
        name="prepare",
    )(padded, *weights, *after)


def collect_kernel(first, width, leads, lead_ref, grad_ref, small_ref, *refs):
    out_ref, extra, sem = refs[-3:]
    cell = lax.broadcasted_iota(jnp.int32, (SPAN, TABLE_PAD), 0)
    lanes = lax.broadcasted_iota(jnp.int32, (SPAN, TABLE_PAD), 1)
    place = (
        (cell // (WLAT * WLON)) * (SPAN_ROW * SPAN_COL)
        + ((cell // WLON) % WLAT) * SPAN_COL
        + cell % WLON
    )
    base = (SPAN_ROW * SPAN_COL) * (LEVELS - 1) + SPAN_COL * (WLAT - 1) + WLON - 1
    spread = (lanes == base - place).astype(F32)
    extra[...] = jnp.zeros_like(extra)
    count = small_ref.shape[1] // width
    sums = jnp.sum(small_ref[...], axis=0, keepdims=True)
    for index in range(count):
        extra[pl.ds(index, 1), :] = sums[:, index * width : (index + 1) * width]
    at = count
    for head in range(HEADS):
        parts = [
            grad_ref[:, pl.ds(head * TILE, TILE)],
            grad_ref[:, pl.ds(HEADS * TILE + head * REST, REST)],
        ]
        wide = jnp.dot(
            jnp.concatenate(parts, axis=1), spread, precision=HIGH, preferred_element_type=F32
        )
        wide = pltpu.roll(wide, 0, 1, stride=1, stride_axis=0)
        total = None
        for group in range(LEVELS * WLAT):
            level, row = divmod(group, WLAT)
            start = level * SPAN_ROW * SPAN_COL + row * SPAN_COL - group * WLON
            part = jnp.sum(wide[group * WLON : (group + 1) * WLON], axis=0, keepdims=True)
            part = pltpu.roll(jnp.broadcast_to(part, (8, TABLE_PAD)), start % TABLE_PAD, 1)
            total = part if total is None else total + part
        for index in range(TABLE_PAD // width):
            extra[pl.ds(at, 1), :] = total[0:1, index * width : (index + 1) * width]
            at += 1
    for index in range(2):
        value = sums[:, (4 + index) * width : (5 + index) * width]
        extra[pl.ds(at + leads * index + lead_ref[0], 1), :] = value
    copy = pltpu.make_async_copy(extra, out_ref.at[pl.ds(first, extra.shape[0]), :], sem)
    copy.start()
    copy.wait()


def collect(lead_index, leads, bias, small, buffer, first, after):
    rows, width = buffer.shape
    return pl.pallas_call(
        functools.partial(collect_kernel, first, width, leads),
        out_shape=jax.ShapeDtypeStruct(buffer.shape, F32),
        in_specs=[SMEM, WHOLE, WHOLE, ANYWHERE] + [ANYWHERE] * len(after),
        out_specs=ANYWHERE,
        scratch_shapes=[VMEM((rows - first, width), F32), pltpu.SemaphoreType.DMA],
        input_output_aliases={3: 0},
        compiler_params=pltpu.CompilerParams(vmem_limit_bytes=LIMIT),
        cost_estimate=SMALL,
        name="collect",
    )(lead_index, bias, small, buffer, *after)


class Peers:
    def __init__(self, lats, leads, rows, send_sems, got_sems):
        self.lead = lax.axis_index("lead")
        lat = lax.axis_index("lat")
        self.core = lax.rem(lat, 2)
        self.chip = lax.div(lat, 2)
        self.chips, self.leads = lats // 2, leads
        self.half = rows // 2
        self.part = self.half // self.chips
        self.piece = self.part // leads
        self.pair = (self.lead, lat + 1 - 2 * self.core)
        self.along_lat = [
            (self.lead, 2 * lax.rem(self.chip + d, self.chips) + self.core)
            for d in range(1, self.chips)
        ]
        self.along_lead = [(lax.rem(self.lead + d, leads), lat) for d in range(1, leads)]
        self.sems = (send_sems, got_sems)
        self.count = 0

    def meet(self, peers):
        barrier = pltpu.get_barrier_semaphore()
        for peer in peers:
            pl.semaphore_signal(
                barrier, inc=1, device_id=peer, device_id_type=pl.DeviceIdType.MESH
            )
        pl.semaphore_wait(barrier, len(peers))

    def send(self, source, target, peer):
        copy = pltpu.make_async_remote_copy(
            src_ref=source,
            dst_ref=target,
            send_sem=self.sems[0].at[self.count],
            recv_sem=self.sems[1].at[self.count],
            device_id=peer,
            device_id_type=pl.DeviceIdType.MESH,
        )
        self.count += 1
        copy.start()
        return copy


def some_rows(start, size):
    return pl.ds(pl.multiple_of(start, 8), size)


def scatter_kernel(lats, leads, in_ref, *refs):
    out_ref, got_pair, sum_pair, got_lat, sum_lat, got_lead, send_sems, got_sems = refs[-8:]
    at = Peers(lats, leads, in_ref.shape[0], send_sems, got_sems)
    at.meet([at.pair] + at.along_lat + at.along_lead)
    at.send(in_ref.at[some_rows((1 - at.core) * at.half, at.half), :], got_pair, at.pair).wait()
    sum_pair[...] = in_ref[some_rows(at.core * at.half, at.half), :] + got_pair[...]
    copies = [
        at.send(
            sum_pair.at[some_rows(lax.rem(at.chip + d, at.chips) * at.part, at.part), :],
            got_lat.at[d - 1],
            at.along_lat[d - 1],
        )
        for d in range(1, at.chips)
    ]
    for copy in copies:
        copy.wait()
    total = sum_pair[some_rows(at.chip * at.part, at.part), :]
    for d in range(1, at.chips):
        total = total + got_lat[d - 1]
    sum_lat[...] = total
    copies = [
        at.send(
            sum_lat.at[some_rows(lax.rem(at.lead + d, leads) * at.piece, at.piece), :],
            got_lead.at[d - 1],
            at.along_lead[d - 1],
        )
        for d in range(1, leads)
    ]
    for copy in copies:
        copy.wait()
    mine = some_rows(at.lead * at.piece, at.piece)
    total = sum_lat[mine, :]
    for d in range(1, leads):
        total = total + got_lead[d - 1]
    out_ref[mine, :] = total
    copies = [at.send(out_ref.at[mine, :], out_ref.at[mine, :], peer) for peer in at.along_lead]
    for copy in copies:
        copy.wait()


def scattered_sum(buffer, after):
    rows, width = buffer.shape
    lats = lax.axis_size("lat")
    leads = lax.axis_size("lead")
    chips = lats // 2
    half = rows // 2
    part = half // chips
    piece = part // leads
    copies = chips + 2 * leads - 2
    return pl.pallas_call(
        functools.partial(scatter_kernel, lats, leads),
        out_shape=jax.ShapeDtypeStruct((part, width), F32),
        in_specs=[WHOLE] + [ANYWHERE] * len(after),
        out_specs=WHOLE,
        scratch_shapes=[
            VMEM((half, width), F32),
            VMEM((half, width), F32),
            VMEM((chips - 1, part, width), F32),
            VMEM((part, width), F32),
            VMEM((leads - 1, piece, width), F32),
            pltpu.SemaphoreType.DMA((copies,)),
            pltpu.SemaphoreType.DMA((copies,)),
        ],
        compiler_params=pltpu.CompilerParams(
            vmem_limit_bytes=LIMIT, collective_id=0, has_side_effects=True
        ),
        cost_estimate=SMALL,
        name="scattered_sum",
    )(buffer, *after)


def hold_kernel(count, *refs):
    for source, target in zip(refs[:count], refs[-count:]):
        target[...] = source[...]


def held_until(arrays, after):
    return pl.pallas_call(
        functools.partial(hold_kernel, len(arrays)),
        out_shape=[jax.ShapeDtypeStruct(array.shape, F32) for array in arrays],
        in_specs=[WHOLE] * len(arrays) + [ANYWHERE] * len(after),
        out_specs=[WHOLE] * len(arrays),
        compiler_params=pltpu.CompilerParams(vmem_limit_bytes=LIMIT),
        cost_estimate=SMALL,
        name="hold",
    )(*arrays, *after)


def gathered(part, after):
    lats = lax.axis_size("lat")
    far = [passed_along(part, "lat", 2 * d) for d in range(1, lats // 2)]
    own = [part] + list(held_until(far, after))
    pairs = [(source, source ^ 1) for source in range(lats)]
    return own, [lax.ppermute(array, "lat", pairs) for array in own]


def finish_kernel(chips, hidden, embed_rows, place_ref, embed_ref, *refs):
    parts, others = refs[:chips], refs[chips : 2 * chips]
    outs, buffer = refs[2 * chips : -1], refs[-1]
    part, width = parts[0].shape
    core, chip = place_ref[0], place_ref[1]
    for index in range(chips):
        at = lax.rem(chip + chips - index, chips) * part
        buffer[some_rows(core * (chips * part) + at, part), :] = parts[index][...]
        buffer[some_rows((1 - core) * (chips * part) + at, part), :] = others[index][...]
    g_mod, g_b_mod, g_qkv, g_table, g_out, g_b_out, g_gain, g_bias, g_up, g_b_up, g_down, g_b_down = outs
    for index in range(3):
        lanes = slice(index * width, (index + 1) * width)
        g_qkv[:, lanes] = buffer[index * width : (index + 1) * width, :]
    g_out[...] = buffer[3 * width : 4 * width, :]
    for index in range(hidden // width):
        lanes = slice(index * width, (index + 1) * width)
        at = 4 * width + index * width
        g_up[:, lanes] = buffer[at : at + width, :]
        at += hidden
        g_down[lanes, :] = buffer[at : at + width, :].T
    at = 4 * width + 2 * hidden
    for place, (target, index) in enumerate(
        [(g_b_down, 0), (g_gain, 0), (g_bias, 0), (g_b_out, 0), (g_b_mod, 0), (g_b_mod, 1)]
        + [(g_b_up, index) for index in range(hidden // width)]
    ):
        target[:, index * width : (index + 1) * width] = buffer[at + place : at + place + 1, :]
    at += 6 + hidden // width
    each = TABLE_PAD // width
    heads = []
    for head in range(HEADS):
        first = at + head * each
        heads.append(
            jnp.concatenate([buffer[first + i : first + i + 1, :] for i in range(each)], axis=1)
        )
    before = lax.broadcasted_iota(jnp.int32, (TABLE_PAD, TABLE_PAD), 0)
    behind = lax.broadcasted_iota(jnp.int32, (TABLE_PAD, TABLE_PAD), 1)
    turn = (before + behind == TABLE_ROWS - 1).astype(F32)
    turned = jnp.dot(
        jnp.concatenate(heads, axis=0), turn, precision=HIGH, preferred_element_type=F32
    )
    g_table[...] = turned[:, :TABLE_ROWS]
    at += HEADS * each
    for index in range(2):
        lanes = slice(index * width, (index + 1) * width)
        rows = buffer[at + index * embed_rows : at + (index + 1) * embed_rows, :]
        g_mod[:, lanes] = jnp.dot(
            embed_ref[...], rows, precision=HIGH, preferred_element_type=F32
        )


def finished(own, others, embeddings, width, hidden):
    chips = len(own)
    lat = lax.axis_index("lat")
    place = jnp.stack([lat % 2, lat // 2]).astype(jnp.int32)
    shapes = [(width, 2 * width), (1, 2 * width), (width, 3 * width), (HEADS, TABLE_ROWS)]
    shapes += [(width, width), (1, width), (1, width), (1, width), (width, hidden), (1, hidden)]
    shapes += [(hidden, width), (1, width)]
    outs = pl.pallas_call(
        functools.partial(finish_kernel, chips, hidden, embeddings.shape[0]),
        out_shape=[jax.ShapeDtypeStruct(shape, F32) for shape in shapes],
        in_specs=[SMEM] + [WHOLE] * (1 + 2 * chips),
        out_specs=[WHOLE] * len(shapes),
        scratch_shapes=[VMEM((2 * chips * own[0].shape[0], width), F32)],
        compiler_params=pltpu.CompilerParams(vmem_limit_bytes=LIMIT),
        cost_estimate=SMALL,
        name="finish",
    )(place, embeddings.T, *own, *others)
    return tuple(out.reshape(-1) if out.shape[0] == 1 else out for out in outs)


def roll_kernel(specs, rows, *refs):
    offsets, own = refs[0], refs[1]
    sems = refs[-1]
    grids = refs[-1 - len(specs) : -1]
    outs = refs[-1 - 2 * len(specs) : -1 - len(specs)]
    copies = []
    for spec, grid in zip(specs, grids):
        started = []
        for place, first, width, halo, halo_first in spec["pieces"]:
            for half in range(2):
                lanes = pl.ds(128 * half, 128)
                cols = pl.ds(place, width)
                for source, begin, target in (
                    (own, first, grid.at[:, pl.ds(0, rows), half, cols, :]),
                    (refs[2 + halo], halo_first, grid.at[:, pl.ds(rows, MARGIN), half, cols, :]),
                ):
                    copy = pltpu.make_async_copy(
                        source.at[:, :, pl.ds(begin, width), lanes],
                        target,
                        sems.at[sum(map(len, copies)) + len(started)],
                    )
                    copy.start()
                    started.append(copy)
        copies.append(started)
    lat_shift = offsets[0]
    lon_shift = offsets[1]
    for spec, grid, out_ref, started in zip(specs, grids, outs, copies):
        for copy in started:
            copy.wait()
        for column in range(spec["count"]):
            start = spec["start"] + column * WLON + lon_shift
            for step in range(rows // WLAT):
                for level in range(LEVELS):
                    for row in range(WLAT):
                        token = step * SPAN + (level * WLAT + row) * WLON
                        for half in range(2):
                            lanes = slice(128 * half, 128 * half + 128)
                            out_ref[column, pl.ds(token, WLON), lanes] = grid[
                                level,
                                lat_shift + step * WLAT + row,
                                half,
                                pl.ds(start, WLON),
                                :,
                            ]


def roll_in(offsets, grid, halos, parts, after):
    rows, cols, features = grid.shape[1:]
    used, specs, scratch, out_shape = [], [], [], []
    for begin, end in parts:
        low = (begin * WLON + 1) // 8 * 8
        high = (end * WLON + WLON - 2) // 8 * 8 + 8
        pieces = []
        for wrap in range(2):
            for first, array in halos:
                left = max(low - wrap * cols, first)
                right = min(high - wrap * cols, first + array.shape[2])
                if left < right:
                    place = left + wrap * cols - low
                    pieces.append((place, left, right - left, len(used), left - first))
                    used.append(array)
        specs.append(dict(pieces=pieces, start=begin * WLON - low, count=end - begin))
        scratch.append(VMEM((LEVELS, rows + MARGIN, 2, high - low, 128), F32))
        shape = (end - begin, rows // WLAT * SPAN, features)
        out_shape.append(jax.ShapeDtypeStruct(shape, F32))
    count = 4 * sum(len(spec["pieces"]) for spec in specs)
    return pl.pallas_call(
        functools.partial(roll_kernel, specs, rows),
        out_shape=out_shape,
        in_specs=[SMEM] + [ANYWHERE] * (1 + len(used) + len(after)),
        out_specs=[WHOLE] * len(parts),
        scratch_shapes=scratch + [pltpu.SemaphoreType.DMA((count,))],
        compiler_params=pltpu.CompilerParams(vmem_limit_bytes=LIMIT),
        cost_estimate=SMALL,
        name="roll_in",
    )(offsets, in_hbm(grid), *used, *after)


def margin_kernel(near, low, cols, first_ref, second_ref, *refs):
    near_ref, far_ref, sems = refs[-3:]
    copies = []
    for index, source in enumerate((first_ref, second_ref)):
        for begin, width, target, place in (
            (0, near, near_ref, 0),
            (low, cols - low, far_ref, 0),
            (0, 16, far_ref, cols - low),
        ):
            copy = pltpu.make_async_copy(
                source.at[:, pl.ds(0, MARGIN), pl.ds(begin, width), :],
                target.at[index, :, :, pl.ds(place, width), :],
                sems.at[len(copies)],
            )
            copy.start()
            copies.append(copy)
    for copy in copies:
        copy.wait()


def margins_of(first, second, near, low, after):
    levels, _, cols, features = first.shape
    return pl.pallas_call(
        functools.partial(margin_kernel, near, low, cols),
        out_shape=[
            jax.ShapeDtypeStruct((2, levels, MARGIN, near, features), F32),
            jax.ShapeDtypeStruct((2, levels, MARGIN, cols - low + 16, features), F32),
        ],
        in_specs=[ANYWHERE] * (2 + len(after)),
        out_specs=[WHOLE] * 2,
        scratch_shapes=[pltpu.SemaphoreType.DMA((6,))],
        compiler_params=pltpu.CompilerParams(vmem_limit_bytes=LIMIT),
        cost_estimate=SMALL,
        name="margins",
    )(in_hbm(first), in_hbm(second), *after)


def unroll_kernel(spec, rows, *refs):
    offsets = refs[0]
    count = spec["count"]
    own = refs[1 : 1 + count]
    tail = refs[1 + count : 1 + 2 * count]
    if spec["targets"]:
        out_hbm, grid, out_ref, sems = refs[-4:]
    else:
        out_ref, grid = refs[-2:]
    lat_shift = offsets[0]
    lon_shift = offsets[1]
    for column in range(count):
        for level in range(LEVELS):
            for row in range(WLAT):
                token = (level * WLAT + row) * WLON
                for half in range(2):
                    lanes = slice(128 * half, 128 * half + 128)
                    cols = pl.ds(column * WLON, WLON)
                    grid[level, row, half, cols, :] = tail[column][0, pl.ds(token, WLON), lanes]
                    for step in range(rows // WLAT):
                        grid[level, WLAT + step * WLAT + row, half, cols, :] = own[column][
                            0, pl.ds(step * SPAN + token, WLON), lanes
                        ]
    start = spec["start"] - lon_shift
    width = spec["width"]
    copies = []
    for level in range(LEVELS):
        for row in range(rows):
            for half in range(2):
                out_ref[level, row, :, 128 * half : 128 * half + 128] = grid[
                    level, WLAT + row - lat_shift, half, pl.ds(start, width), :
                ]
        for place, first, size in spec["targets"]:
            copy = pltpu.make_async_copy(
                out_ref.at[level, :, pl.ds(place, size), :],
                out_hbm.at[level, :, pl.ds(first, size), :],
                sems.at[len(copies)],
            )
            copy.start()
            copies.append(copy)
    for copy in copies:
        copy.wait()


def targets_of(start, end, cols):
    edge = min(end, cols)
    return [(0, start, edge - start)] + ([(cols - start, 0, end - cols)] if end > cols else [])


def roll_back(offsets, own, tail, first, start, end, shape, after, into=()):
    count = len(own)
    levels, rows, cols, features = shape
    tokens = own[0][0].shape[1]
    width = end - start
    spec = dict(count=count, start=start - first, width=width)
    spec["targets"] = targets_of(start, end, cols) if into else []

    def spec_of(entry, tall):
        index, lane = (entry[1:] + (0,))[:2]
        return pl.BlockSpec((1, tall, features), lambda i: (index, 0, lane))

    scratch = [VMEM((levels, rows + WLAT, 2, count * WLON + 16, 128), F32)]
    piece = (levels, rows, width, features)
    base = [array for array in into if array is not None]
    if into:
        out_shape, out_spec = shape, ANYWHERE
        scratch += [VMEM(piece, F32), pltpu.SemaphoreType.DMA((2 * levels,))]
    else:
        out_shape, out_spec = piece, pl.BlockSpec(piece, lambda i: (0, 0, 0, 0))
    return pl.pallas_call(
        functools.partial(unroll_kernel, spec, rows),
        out_shape=(pltpu.HBM if into else jax.ShapeDtypeStruct)(out_shape, F32),
        grid=(1,),
        in_specs=[SMEM]
        + [spec_of(entry, tokens) for entry in own]
        + [spec_of(entry, SPAN) for entry in tail]
        + [ANYWHERE] * (len(base) + len(after)),
        out_specs=out_spec,
        scratch_shapes=scratch,
        input_output_aliases={1 + 2 * count: 0} if base else {},
        compiler_params=pltpu.CompilerParams(vmem_limit_bytes=LIMIT),
        cost_estimate=SMALL,
        name="roll_back",
    )(
        offsets,
        *[in_hbm(entry[0]) for entry in own],
        *[entry[0] for entry in tail],
        *[in_hbm(array) for array in base],
        *after,
    )


def place_kernel(targets, piece_hbm, *refs):
    out_hbm, held, sems = refs[-3:]
    inward, outward = [], []
    for level in range(LEVELS):
        copy = pltpu.make_async_copy(piece_hbm.at[level], held.at[level], sems.at[level])
        copy.start()
        inward.append(copy)
    for level in range(LEVELS):
        inward[level].wait()
        for place, first, size in targets:
            copy = pltpu.make_async_copy(
                held.at[level, :, pl.ds(place, size), :],
                out_hbm.at[level, :, pl.ds(first, size), :],
                sems.at[LEVELS + len(outward)],
            )
            copy.start()
            outward.append(copy)
    for copy in outward:
        copy.wait()


def placed_in(grid, piece, start, shape, after):
    targets = targets_of(start, start + piece.shape[2], shape[2])
    base = [] if grid is None else [grid]
    return pl.pallas_call(
        functools.partial(place_kernel, targets),
        out_shape=pltpu.HBM(shape, F32),
        in_specs=[ANYWHERE] * (1 + len(base) + len(after)),
        out_specs=ANYWHERE,
        scratch_shapes=[VMEM(piece.shape, F32), pltpu.SemaphoreType.DMA((3 * LEVELS,))],
        input_output_aliases={1: 0} if base else {},
        compiler_params=pltpu.CompilerParams(vmem_limit_bytes=LIMIT),
        cost_estimate=SMALL,
        name="place",
    )(piece, *[in_hbm(array) for array in base], *after)


def row_sums(value):
    return jnp.sum(value.reshape(value.shape[0] // 8, 8, value.shape[1]), axis=0)


def block_kernel(
    begin,
    halo_first,
    given,
    waits,
    offsets,
    recv_ref,
    earlier_hbm,
    cot_hbm,
    halo_hbm,
    live_ref,
    mod_ref,
    w_qkv_ref,
    w_qkv_t_ref,
    bias_ref,
    w_out_ref,
    w_out_t_ref,
    vec_ref,
    w_up_ref,
    w_up_t_ref,
    b_up_ref,
    w_down_ref,
    w_down_t_ref,
    *refs,
):
    (
        res_ref,
        grad_ref,
        tail_ref,
        acc_main,
        acc_bias,
        acc_small,
        fetched,
        sems,
        x_s,
        g_s,
        normed_s,
        inv_s,
        ln_in_s,
        proj_s,
        prob_s,
        prob_low_s,
        q_wide_s,
        d_wide_s,
        dscore_s,
        q_wide_t,
        d_wide_t,
        att_t,
        dq_t,
        ln_two_s,
        act_s,
        dhid_s,
        branch_s,
        attg_s,
        gproj_s,
        att_s,
        gatt_s,
        normed_two_s,
        inv_two_s,
        first_s,
        pre_s,
        back_s,
        turned_one,
        turned_two,
    ) = refs[given + waits :]
    width = recv_ref.shape[-1]
    tokens = recv_ref.shape[1]
    count = tokens // SPAN
    hidden = w_up_ref.shape[1]
    head_size = width // HEADS
    wide = HEADS * SPAN
    scale = head_size ** (-0.5)

    @pl.when(pl.program_id(0) == 0)
    def _():
        for index, target in enumerate((acc_main, acc_bias, acc_small)):
            target[...] = refs[index][...] if given else jnp.zeros_like(target)

    step = pl.program_id(0)
    grid_rows = earlier_hbm.shape[1]
    grid_cols = earlier_hbm.shape[2]
    lat_shift = offsets[0]
    lon_shift = offsets[1]

    def place_of(at):
        first = (begin + at) * WLON + lon_shift
        return first // 8 * 8, first % 8

    def copies_of(at, slot):
        first, _ = place_of(at)
        whole, split = [], []
        for index, source in enumerate((earlier_hbm, cot_hbm)):
            for half in range(2):
                lanes = pl.ds(128 * half, 128)
                own = fetched.at[slot, index, :, pl.ds(0, grid_rows), half]
                sem = sems.at[slot, 4 * index + 2 * half]
                cols = pl.ds(pl.multiple_of(first, 8), REACH)
                whole.append((source.at[:, :, cols, lanes], own, sem))
                for j in range(0, REACH, 8):
                    cols = pl.ds(pl.multiple_of((first + j) % grid_cols, 8), 8)
                    split.append((source.at[:, :, cols, lanes], own.at[:, :, pl.ds(j, 8), :], sem))
        return whole, split

    def halo_copies_of(at, slot):
        first, _ = place_of(at)
        cols = pl.ds(pl.multiple_of(first - halo_first, 8), REACH)
        copies = []
        for index in range(2):
            for half in range(2):
                copies.append(
                    (
                        halo_hbm.at[index, :, :, cols, pl.ds(128 * half, 128)],
                        fetched.at[slot, index, :, pl.ds(grid_rows, MARGIN), half],
                        sems.at[slot, 4 * index + 2 * half + 1],
                    )
                )
        return copies

    def fetch(at, slot):
        first, _ = place_of(at)
        whole, split = copies_of(at, slot)

        @pl.when(first + REACH <= grid_cols)
        def _():
            for copy in whole:
                pltpu.make_async_copy(*copy).start()

        @pl.when(first + REACH > grid_cols)
        def _():
            for copy in split:
                pltpu.make_async_copy(*copy).start()

        for copy in halo_copies_of(at, slot):
            pltpu.make_async_copy(*copy).start()

    slot = step % 2

    @pl.when(step == 0)
    def _():
        fetch(0, 0)

    @pl.when(step + 1 < pl.num_programs(0))
    def _():
        fetch(step + 1, 1 - slot)

    for source, target, sem in copies_of(0, slot)[0] + halo_copies_of(0, slot):
        pltpu.make_async_copy(source, target, sem).wait()
    _, inside = place_of(step)
    for index, target in enumerate((x_s, g_s)):
        for part in range(count):
            for level in range(LEVELS):
                for row in range(WLAT):
                    token = part * SPAN + (level * WLAT + row) * WLON
                    for half in range(2):
                        target[pl.ds(token, WLON), 128 * half : 128 * half + 128] = fetched[
                            slot, index, level, lat_shift + part * WLAT + row, half, pl.ds(inside, WLON), :
                        ]

    shift_one = mod_ref[0:1, :]
    gain_one = mod_ref[1:2, :]
    b_out = vec_ref[0:1, :]
    gain_two = vec_ref[1:2, :]
    bias_two = vec_ref[2:3, :]
    b_down = vec_ref[3:4, :]

    group = 128 // head_size
    groups = [
        (slice(first * TILE, (first + group) * TILE), slice(first * head_size, first * head_size + 128))
        for first in range(0, HEADS, group)
    ]
    rest = slice(HEADS * TILE, wide)

    @pl.when(step == 0)
    def _():
        for part in range(count):
            for lanes, own in groups + [(rest, slice(0, width))]:
                for target in (q_wide_s, d_wide_s):
                    target[part, lanes, own] = jnp.zeros_like(target[part, lanes, own])
                for target in (q_wide_t, d_wide_t):
                    target[part, own, lanes] = jnp.zeros_like(target[part, own, lanes])

    def spread_heads(value, turned, target, target_t):
        for head in range(HEADS):
            own = slice(head * head_size, (head + 1) * head_size)
            tile = pl.ds(head * TILE, TILE)
            rest = pl.ds(HEADS * TILE + head * REST, REST)
            target[tile, own] = value[:TILE, own]
            target[rest, own] = value[TILE:, own]
            target_t[own, tile] = turned[own, :TILE]
            target_t[own, rest] = turned[own, TILE:]

    def head_products(turned, scores, target):
        last = dot_nn(turned, scores[:, pl.ds(HEADS * TILE, HEADS * REST)])
        for head in range(HEADS):
            own = slice(head * head_size, (head + 1) * head_size)
            first = dot_nn(turned[own, :], scores[:, pl.ds(head * TILE, TILE)])
            target[own, 0:TILE] = first.astype(BF16)
            target[own, TILE:SPAN] = last[own, head * REST : (head + 1) * REST].astype(BF16)

    def wide_product(left, wide_t, start, size):
        features = slice(0, width)
        if start < rest.start:
            features = groups[start // (group * TILE)][1]
        return dot_nn(left[:, features], wide_t[features, start : start + size])

    def wide_sum(scores, wide_s):
        parts = [dot_nn(scores[:, lanes], wide_s[lanes, own]) for lanes, own in groups]
        return jnp.concatenate(parts, axis=1) + dot_nn(scores[:, rest], wide_s[rest, :])

    everything = count * SPAN
    blocks = [slice(start, start + BLOCK) for start in range(0, everything, BLOCK)]
    items = [
        (part, start, min(WIDE, wide - start))
        for part in range(count)
        for start in range(0, wide, WIDE)
    ]

    def rows_of(part):
        return slice(part * SPAN, (part + 1) * SPAN)

    def ahead(products, work):
        held = products[0]()
        for index in range(len(products)):
            later = products[index + 1]() if index + 1 < len(products) else None
            work(index, held)
            held = later

    def normalized(value):
        centered = value - jnp.mean(value, axis=-1, keepdims=True)
        inv = lax.rsqrt(jnp.mean(centered * centered, axis=-1, keepdims=True) + EPS)
        return centered * inv, inv

    def norm_back(hat, normed, inv):
        first = jnp.mean(hat, axis=-1, keepdims=True)
        second = jnp.mean(hat * normed, axis=-1, keepdims=True)
        return inv * (hat - first - normed * second)

    def add_small(place, values):
        acc_small[:, place * width : (place + 1) * width] += functools.reduce(jnp.add, values)

    for rows in blocks:
        x = recv_ref[0, rows, :] + x_s[rows, :]
        x_s[rows, :] = x
        normed, inv = normalized(x)
        normed_s[rows, :] = normed
        inv_s[rows, :] = inv
        ln_in_s[rows, :] = (normed * gain_one + shift_one).astype(BF16)
    for start in range(0, 3 * width, WIDE):
        lanes = slice(start, min(start + WIDE, 3 * width))
        proj_s[:, lanes] = dot_nn(ln_in_s[...], w_qkv_ref[:, lanes]).astype(BF16)

    live = []
    for part in range(count):
        rows = rows_of(part)
        live.append(jnp.broadcast_to(live_ref[0, rows, :], (SPAN, 128)))
        queries = proj_s[rows, 0:width]
        spread_heads(queries, queries.T, q_wide_s.at[part], q_wide_t.at[part])

    def raw_scores(item):
        part, start, size = item
        keys = proj_s[rows_of(part), width : 2 * width]
        return wide_product(keys, q_wide_t.at[part], start, size)

    def softmax(index, raw):
        part, start, size = items[index]
        for place in range(0, size, 128):
            lanes = slice(start + place, start + place + 128)
            scores = raw[:, place : place + 128] * (scale * LOG2E) + bias_ref[:, lanes]
            scores = jnp.where(live[part] > 0.5, scores, NEG)
            expo = jnp.exp2(scores - jnp.max(scores, axis=0, keepdims=True))
            prob = expo * (1.0 / jnp.sum(expo, axis=0, keepdims=True))
            prob_s[part, :, lanes] = prob
            prob_low_s[part, :, lanes] = prob.astype(BF16)
        if start + size == wide:
            values_t = proj_s[rows_of(part), 2 * width : 3 * width].T
            head_products(values_t, prob_low_s.at[part], att_t.at[part])

    ahead([functools.partial(raw_scores, item) for item in items], softmax)

    for part in range(count):
        att_s[rows_of(part), :] = att_t[part].T
    first_s[...] = dot_nn(att_s[...], w_out_ref[...])
    for rows in blocks:
        mid = x_s[rows, :] + first_s[rows, :] + b_out
        x_s[rows, :] = mid
        normed, inv = normalized(mid)
        normed_two_s[rows, :] = normed
        inv_two_s[rows, :] = inv
        ln_two_s[rows, :] = (normed * gain_two + bias_two).astype(BF16)
        branch_s[rows, :] = g_s[rows, :].astype(BF16)

    def feed(start):
        lanes = slice(start, start + WIDE)
        slot = start // WIDE % 2
        pre_s[slot] = dot_nn(ln_two_s[...], w_up_ref[:, lanes])
        back_s[slot] = dot_nn(branch_s[...], w_down_t_ref[:, lanes])

    def gelu(index, _):
        for first in range(0, WIDE, width):
            gelu_part(index * WIDE + first, index % 2, slice(first, first + width))

    def gelu_part(start, slot, inside):
        lanes = slice(start, start + width)
        sums = []
        for rows in blocks:
            pre = pre_s[slot, rows, inside] + b_up_ref[:, lanes]
            square = pre * pre
            half = 0.5 + 0.5 * jnp.tanh(pre * (GELU_ONE + GELU_TWO * square))
            act_s[rows, lanes] = (pre * half).astype(BF16)
            slope = pre * (2 * GELU_ONE + (6 * GELU_TWO) * square)
            dhid = back_s[slot, rows, inside] * (half * (1.0 + (1.0 - half) * slope))
            dhid = dhid.astype(BF16)
            dhid_s[rows, lanes] = dhid
            sums.append(row_sums(dhid.astype(F32)))
        add_small(6 + start // width, sums)

    ahead([functools.partial(feed, start) for start in range(0, hidden, WIDE)], gelu)

    first_s[...] = dot_nn(dhid_s[...], w_up_t_ref[...])
    res_ref[0] = dot_nn(act_s[...], w_down_ref[...])
    sums = [[], [], [], []]
    for rows in blocks:
        g_ln = first_s[rows, :]
        normed = normed_two_s[rows, :]
        grad_mid = g_s[rows, :] + norm_back(g_ln * gain_two, normed, inv_two_s[rows, :])
        grad_ref[0, rows, :] = grad_mid
        att_grad = grad_mid.astype(BF16)
        attg_s[rows, :] = att_grad
        for place, value in enumerate(
            (branch_s[rows, :].astype(F32), g_ln * normed, g_ln, att_grad.astype(F32))
        ):
            sums[place].append(row_sums(value))
    for place in range(4):
        add_small(place, sums[place])

    gatt_s[...] = dot_nn(attg_s[...], w_out_t_ref[...]).astype(BF16)
    for rows in blocks:
        result = res_ref[0, rows, :] + x_s[rows, :] + b_down
        res_ref[0, rows, :] = result
        if rows.start >= (count - 1) * SPAN:
            start = rows.start - (count - 1) * SPAN
            tail_ref[0, start : start + BLOCK, 0:width] = result
    for part in range(count):
        g_att = gatt_s[rows_of(part), :]
        spread_heads(g_att, g_att.T, d_wide_s.at[part], d_wide_t.at[part])

    def add_main(place, total):
        acc_main[place * width : (place + 1) * width, :] += total

    def out_gradient():
        total = dot_nn(att_t[0], attg_s[rows_of(0), :])
        for part in range(1, count):
            total += dot_nn(att_t[part], attg_s[rows_of(part), :])
        add_main(3, total)

    def feed_gradient(place, left, right, start):
        total = dot_nn(left[...], right[:, start : start + WIDE])
        for first in range(0, total.shape[1], width):
            add_main(place + first // width, total[:, first : first + width])

    turned_one[...] = ln_two_s[...].T
    turned_two[...] = branch_s[...].T
    extra = [out_gradient]
    for start in range(0, hidden, WIDE):
        place = 4 + start // width
        extra.append(functools.partial(feed_gradient, place, turned_one, dhid_s, start))
    for start in range(0, hidden, WIDE):
        place = 4 + (hidden + start) // width
        extra.append(functools.partial(feed_gradient, place, turned_two, act_s, start))

    def d_probs(item):
        part, start, size = item
        values = proj_s[rows_of(part), 2 * width : 3 * width]
        return wide_product(values, d_wide_t.at[part], start, size)

    def d_scores(index, d_prob):
        part, start, size = items[index]
        rows = rows_of(part)
        if extra:
            extra.pop(0)()
        for place in range(0, size, 128):
            lanes = slice(start + place, start + place + 128)
            own = d_prob[:, place : place + 128]
            prob = prob_s[part, :, lanes]
            inside = jnp.sum(own * prob, axis=0, keepdims=True)
            d_score = prob * (own - inside)
            acc_bias[:, lanes] += d_score
            dscore_s[part, :, lanes] = (d_score * scale).astype(BF16)
        if start + size == wide:
            d_values = wide_sum(prob_low_s.at[part], d_wide_s.at[part])
            d_keys = wide_sum(dscore_s.at[part], q_wide_s.at[part])
            keys_t = proj_s[rows, width : 2 * width].T
            head_products(keys_t, dscore_s.at[part], dq_t.at[part])
            gproj_s[rows, 0:width] = dq_t[part].T
            gproj_s[rows, width : 2 * width] = d_keys.astype(BF16)
            gproj_s[rows, 2 * width : 3 * width] = d_values.astype(BF16)

    ahead([functools.partial(d_probs, item) for item in items], d_scores)
    for rest in extra:
        rest()

    first_s[...] = dot_nn(gproj_s[...], w_qkv_t_ref[...])
    turned_one[...] = ln_in_s[...].T
    for start in range(0, 3 * width, WIDE):
        feed_gradient(start // width, turned_one, gproj_s, start)
    sums = [[], []]
    for rows in blocks:
        g_ln = first_s[rows, :]
        normed = normed_s[rows, :]
        total = grad_ref[0, rows, :] + norm_back(g_ln * gain_one, normed, inv_s[rows, :])
        grad_ref[0, rows, :] = total
        if rows.start >= (count - 1) * SPAN:
            start = rows.start - (count - 1) * SPAN
            tail_ref[0, start : start + BLOCK, width : 2 * width] = total
        sums[0].append(row_sums(g_ln))
        sums[1].append(row_sums(g_ln * normed))
    for place in range(2):
        add_small(4 + place, sums[place])


def run_block(
    offsets, begin, received, earlier, cot, halo, halo_first, live, fixed, sums, sum_shapes, after
):
    columns, tall, width = received.shape
    count = tall // SPAN
    hidden = fixed[7].shape[1]
    wide = HEADS * SPAN
    rows = earlier.shape[1]

    def moving(tall_size, last, first=0):
        return pl.BlockSpec((1, tall_size, last), lambda i: (i + first, 0, 0))

    def still(array):
        place = (0,) * len(array.shape)
        return pl.BlockSpec(array.shape, lambda i: place, pipeline_mode=pl.Buffered(1))

    in_specs = [SMEM, moving(tall, width)] + [ANYWHERE] * 3 + [moving(tall, 1, begin)]
    first_sum = len(in_specs) + len(fixed)
    in_specs += [still(array) for array in fixed] + [still(array) for array in sums]
    in_specs += [ANYWHERE] * len(after)
    shapes = [pltpu.HBM(sum_shapes[0], F32)]
    shapes += [jax.ShapeDtypeStruct(shape, F32) for shape in sum_shapes[1:]]
    out_specs = [moving(tall, width)] * 2 + [moving(SPAN, 2 * width)] + [still(a) for a in shapes]
    out_shape = (
        [pltpu.HBM((columns, tall, width), F32)] * 2
        + [jax.ShapeDtypeStruct((columns, SPAN, 2 * width), F32)]
        + shapes
    )
    return pl.pallas_call(
        functools.partial(block_kernel, begin, halo_first, len(sums), len(after)),
        out_shape=out_shape,
        grid=(columns,),
        in_specs=in_specs,
        out_specs=out_specs,
        scratch_shapes=[
            VMEM((2, 2, LEVELS, rows + MARGIN, 2, 24, 128), F32),
            pltpu.SemaphoreType.DMA((2, 8)),
            VMEM((tall, width), F32),
            VMEM((tall, width), F32),
            VMEM((tall, width), F32),
            VMEM((tall, 1), F32),
            VMEM((tall, width), BF16),
            VMEM((tall, 3 * width), BF16),
            VMEM((count, SPAN, wide), F32),
            VMEM((count, SPAN, wide), BF16),
            VMEM((count, wide, width), BF16),
            VMEM((count, wide, width), BF16),
            VMEM((count, SPAN, wide), BF16),
            VMEM((count, width, wide), BF16),
            VMEM((count, width, wide), BF16),
            VMEM((count, width, SPAN), BF16),
            VMEM((count, width, SPAN), BF16),
            VMEM((tall, width), BF16),
            VMEM((tall, hidden), BF16),
            VMEM((tall, hidden), BF16),
            VMEM((tall, width), BF16),
            VMEM((tall, width), BF16),
            VMEM((tall, 3 * width), BF16),
            VMEM((tall, width), BF16),
            VMEM((tall, width), BF16),
            VMEM((tall, width), F32),
            VMEM((tall, 1), F32),
            VMEM((tall, width), F32),
            VMEM((2, tall, WIDE), F32),
            VMEM((2, tall, WIDE), F32),
            VMEM((width, tall), BF16),
            VMEM((width, tall), BF16),
        ],
        input_output_aliases={first_sum + i: 3 + i for i in range(len(sums))},
        compiler_params=pltpu.CompilerParams(vmem_limit_bytes=BLOCK_LIMIT),
        cost_estimate=pl.CostEstimate(
            flops=columns * 10**10, bytes_accessed=1, transcendentals=0
        ),
        name="block",
    )(offsets, received, in_hbm(earlier), in_hbm(cot), halo, live, *fixed, *sums, *after)


def window_tokens(grid):
    shape = grid.shape
    blocks = grid.reshape((shape[0], shape[1] // WLAT, WLAT, shape[2] // WLON, WLON))
    return blocks.transpose((3, 1, 0, 2, 4)).reshape((shape[2] // WLON, -1, 1))


SHARES = (4, 4, 4, 4)


def on_device(
    state,
    earlier,
    cotangent,
    level_mask,
    window_offsets,
    lead_index,
    embeddings,
    w_mod,
    b_mod,
    w_qkv,
    bias_table,
    w_out,
    b_out,
    norm_gain,
    norm_bias,
    w_up,
    b_up,
    w_down,
    b_down,
):
    width = state.shape[-1]
    rows = state.shape[2]
    cols = state.shape[3]
    hidden = w_up.shape[1]
    total = cols // WLON
    offsets = window_offsets[0]
    lat_shift = offsets[0]
    lon_shift = offsets[1]
    ends = [int(total * share) // sum(SHARES) for share in np.cumsum(SHARES)]
    steps = list(zip([0] + ends[:-1], ends))
    near = ((ends[0] - 1) * WLON + WLON - 1) // 8 * 8 + REACH
    far = (ends[0] * WLON + 1) // 8 * 8

    next_offsets = passed_along(offsets, "lead", -1)
    state_halos = [
        (low, passed_along(state[0][:, :MARGIN, low:high], "lat", -1))
        for low, high in ((0, near), (near, cols))
    ]
    grid_live = level_mask[0].astype(F32)
    live_halo = passed_along(grid_live[:, :MARGIN], "lat", -1)
    moved = []
    for step in steps:
        moved += roll_in(next_offsets, state[0], state_halos, [step], moved[-1:] or [live_halo])
    received = [passed_along(array, "lead", 1) for array in moved]
    margins = margins_of(earlier[0], cotangent[0], near, far, moved[:1])
    halos = [passed_along(margin, "lat", -1) for margin in margins]

    extended = jnp.concatenate([grid_live, live_halo], axis=1)
    shifted = lax.dynamic_slice_in_dim(extended, lat_shift, rows, 1)
    doubled = jnp.concatenate([shifted, shifted], axis=2)
    live = window_tokens(lax.dynamic_slice_in_dim(doubled, lon_shift, cols, 2))

    emb_row = lax.dynamic_index_in_dim(embeddings, lead_index[0], 0, keepdims=False)
    modulation = jnp.dot(emb_row, w_mod, precision=HIGH) + b_mod
    mod = jnp.stack([modulation[:width], 1.0 + modulation[width:]])
    vectors = jnp.stack([b_out, norm_gain, norm_bias, b_down])
    bias, w_qkv_t, w_out_t, w_up_t, w_down_t = prepare(
        bias_table, [w_qkv, w_out, w_up, w_down], moved[1:2]
    )
    fixed = [
        mod,
        in_hbm(w_qkv),
        in_hbm(w_qkv_t),
        in_hbm(bias),
        in_hbm(w_out),
        in_hbm(w_out_t),
        vectors,
        in_hbm(w_up),
        in_hbm(w_up_t),
        b_up[None],
        in_hbm(w_down),
        in_hbm(w_down_t),
    ]
    main_rows = 4 * width + 2 * hidden
    few = 6 * width + hidden
    table_rows = HEADS * TABLE_PAD // width
    mod_rows = 2 * embeddings.shape[0]
    used = main_rows + few // width + table_rows + mod_rows
    unit = 8 * lax.axis_size("lat") * lax.axis_size("lead")
    buffer_rows = -(-used // unit) * unit
    sum_shapes = [(buffer_rows, width), (SPAN, HEADS * SPAN), (8, few)]
    sums = []

    results, grads = [], []
    shape = earlier.shape[1:]

    def back(kept, start, end, after, into=()):
        low = (start - (WLON - 1)) // WLON
        high = (end - 2) // WLON
        picked = [kept[window % total] for window in range(low, high + 1)]
        own, tail = zip(*picked)
        return roll_back(offsets, own, tail, low * WLON, start, end, shape, after, into)

    bounds = [(end * WLON + 1) // 8 * 8 for end in ends[:-1]] + [cols + 16]
    pieces = list(zip([16] + bounds[:-1], bounds))
    rolled, sent = [], []

    def send(start, end, after):
        rolled.append(back(grads, start, end, after))
        sent.append((passed_along(rolled[-1], "lead", -1), start))

    for index, (begin, end) in enumerate(steps):
        made = run_block(
            offsets,
            begin,
            received[index],
            earlier[0],
            cotangent[0],
            halos[min(index, 1)],
            0 if index == 0 else far,
            live,
            fixed,
            sums,
            sum_shapes,
            moved[1:2] if index == 0 else rolled[-1:],
        )
        sums = made[3:]
        tail = passed_along(made[2], "lat", 1)
        for window in range(begin, end):
            results.append(((made[0], window - begin), (tail, window - begin, 0)))
            grads.append(((made[1], window - begin), (tail, window - begin, 1)))
        if index == len(steps) - 2:
            send(pieces[0][0], pieces[index - 1][1], [made[4]])
    send(*pieces[-2], [made[4]])
    buffer = collect(lead_index, embeddings.shape[0], sums[1], sums[2], sums[0], main_rows, rolled[-1:])
    part = scattered_sum(buffer, [])
    early = len(sent)
    middle = (pieces[-1][0] + pieces[-1][1]) // 16 * 8
    send(pieces[-1][0], middle, [part] + [piece for piece, _ in sent])
    send(middle, pieces[-1][1], rolled[-1:])
    block_out = back(results, pieces[0][0], pieces[-3][1], rolled[-1:], (None,))
    block_out = back(results, pieces[-2][0], pieces[-1][1], [], (block_out,))
    state_grad, after = None, [in_hbm(block_out)]
    for piece, start in sent[:early]:
        state_grad = placed_in(state_grad, piece, start, shape, after)
        after = []
    own, others = gathered(part, [in_hbm(state_grad)])
    for piece, start in sent[early:]:
        state_grad = placed_in(state_grad, piece, start, shape, [])
    outs = finished(own, others, embeddings, width, hidden)
    return (block_out[None], state_grad[None]) + outs


def solution(mesh):
    grid = P("lead", None, "lat", None, None)
    placed = (grid, grid, grid, P("lead", None, "lat", None), P("lead", None), P("lead"))
    return jax.shard_map(
        on_device,
        mesh=mesh,
        in_specs=placed + (P(),) * 13,
        out_specs=(grid, grid) + (P(),) * 12,
        check_vma=False,
    )
```
